512 devices in a mesh: leaf: 512 (over z, x, y, core).
Axes of the slice: x: 4, y: 8, z: 8, core: 2. Of those that a mesh axis runs over, the one named last changes fastest.
Arguments:
- rhs: bfloat16 [256, 1048576], P(None, 'leaf'), may hold values from -6 to 6
- bases: bfloat16 [5, 128, 1048576], P(None, None, 'leaf'), may hold values from -13 to 13
- coupling: bfloat16 [5, 512, 128, 256], P(None, 'leaf'), may hold values from -1 to 1, as said below
Outputs:
- whitened: bfloat16 [256, 1048576], P(None, 'leaf')
The draws below stay inside these ranges and needn't reach their ends.
Inputs may be any that keep to these rules, and one draw needn't show every extreme that they name: coupling[l, d] is the same for all devices d of one child block at level l, the aligned blocks of 512 // 2**(l+1) devices.
All inputs are finite; a program needn't handle non-finite values.
Results may differ from the reference program's by a relative error of at most 0.029.
Values may be sent and summed in bfloat16 or wider, within the bound.
No kernel may reach another device: no remote copies, remote signals or barrier semaphores. Data moves between devices by JAX's collectives and lax.ppermute only.
A program may use at most 64 MiB of HBM per device.

```python
import jax
import jax.numpy as jnp
from jax import lax

P_DEV = 2048
NRHS = 256
R = 128
LEVELS = 5
LEAVES = 512
POINTS = 1048576


def draw_bases(key, part):
    key = jax.random.fold_in(key, 11)
    first, second = jax.random.split(key)
    values = jnp.clip(jax.random.normal(first, (LEVELS, R, POINTS), jnp.float32), -4.0, 4.0)
    scales = jnp.exp(jax.random.uniform(second, (LEVELS, 1, POINTS), jnp.float32, -1.15, 1.15))
    return (values * scales).astype(jnp.bfloat16)


def draw_coupling(key, part):
    key = jax.random.fold_in(key, 23)
    levels_out = []
    for level in range(LEVELS):
        count = 2 ** (level + 1)
        group = LEAVES // count
        sigma = 0.5 / (R * (2.0 * P_DEV * group) ** 0.5 * 2.15)
        base = jnp.clip(jax.random.normal(jax.random.fold_in(key, level), (count, R, 2 * R), jnp.float32), -4.0, 4.0)
        levels_out.append(jnp.repeat(base * sigma, group, axis=0))
    return jnp.stack(levels_out).astype(jnp.bfloat16)


def block_levels(key, shape, shards, smallest, largest):
    def one(position, shards_of):
        draws = jax.random.uniform(jax.random.fold_in(jax.random.fold_in(key, 6), position), (shards_of,), jnp.float32, smallest / len(shards), largest / len(shards))
        return jnp.repeat(jnp.exp(draws), shape[position] // shards_of).reshape((-1,) + (1,) * (len(shape) - position - 1))

    loudness = one(*shards[0])
    for cut in shards[1:]:
        loudness = loudness * one(*cut)
    return loudness


def normal_values(key, shape, scale, limit, cuts=(), dtype=jnp.bfloat16):
    entries = jax.random.normal(key, shape, jnp.float32) * scale
    if len(cuts) > 0:
        entries = block_levels(key, shape, cuts, -0.22, 0.18) * entries
    return jnp.clip(entries, min=-limit, max=limit).astype(dtype)


def setup_inputs(seed: int = 0) -> dict:
    key_of = jax.random.split(jax.random.key(seed), 4)
    return {
        "rhs": normal_values(key_of[0], (NRHS, POINTS), 1.0, 6.0, ((1, 512),)),
        "bases": draw_bases(jax.random.fold_in(key_of[3], 71), 0),
        "coupling": draw_coupling(jax.random.fold_in(key_of[3], 71), 0),
    }


def reference(rhs, bases, coupling):
    state = rhs.astype(jnp.float32)
    for level in reversed(range(LEVELS)):
        count = 2 ** (level + 1)
        width = POINTS // count
        group = LEAVES // count
        rounded = lax.optimization_barrier(state.astype(jnp.bfloat16)).astype(jnp.float32)
        basis = bases[level].astype(jnp.float32).reshape(R, count, width)
        proj = jnp.einsum('ncp,rcp->cnr', rounded.reshape(NRHS, count, width), basis)
        pair = proj.reshape(count // 2, 2, NRHS, R).transpose(0, 2, 1, 3).reshape(count // 2, NRHS, 2 * R)
        pair = lax.optimization_barrier(pair.astype(jnp.bfloat16)).astype(jnp.float32)
        pair = jnp.repeat(pair, 2, axis=0)
        blocks = coupling[level, ::group].astype(jnp.float32)
        corr = jnp.einsum('cnk,crk->cnr', pair, blocks)
        corr = lax.optimization_barrier(corr.astype(jnp.bfloat16)).astype(jnp.float32)
        update = jnp.einsum('cnr,rcp->ncp', corr, basis).reshape(NRHS, POINTS)
        state = state - update
    return state.astype(jnp.bfloat16)
```

```python
import functools

import jax
import jax.numpy as jnp
from jax import lax
from jax.experimental import pallas as pl
from jax.experimental.pallas import tpu as pltpu
from jax.sharding import Mesh
from jax.sharding import PartitionSpec as P


ROWS = 16
PIECES = 5
R = 128
STEPS = 4
F32 = jnp.float32
BF16 = jnp.bfloat16
VMEM_LIMIT = 40 * 1024 * 1024


def dot_t(a, b):
    return lax.dot_general(a, b, (((1,), (1,)), ((), ())), preferred_element_type=F32)


def dot(a, b):
    return jnp.dot(a, b, preferred_element_type=F32)


def project_kernel(rhs, bases, out, acc_p, acc_a, acc_b, acc_c, acc_d):
    step = pl.program_id(0)

    @pl.when(step == 0)
    def _():
        for acc in (acc_p, acc_a, acc_b, acc_c, acc_d):
            acc[...] = jnp.zeros_like(acc)

    width = rhs.shape[1]
    everything = bases[...].reshape(5 * R, width)
    acc_p[...] += dot_t(rhs[...], everything)
    acc_a[...] += dot_t(everything[: 3 * R], everything[3 * R :])
    acc_b[...] += dot_t(everything[:R], everything[R : 3 * R])
    acc_c[...] += dot_t(everything[3 * R : 4 * R], everything[4 * R :])
    acc_d[...] += dot_t(everything[R : 2 * R], everything[2 * R : 3 * R])

    @pl.when(step == STEPS - 1)
    def _():
        def put(position, value):
            out[:, ROWS * position : ROWS * (position + 1), :] = value.astype(BF16).reshape(16, ROWS, R)

        for level in range(5):
            put(level, acc_p[:, R * level : R * (level + 1)])
        put(5, acc_a[: 2 * R, R:])
        put(6, jnp.concatenate([acc_a[2 * R :, R:], acc_c[...]], axis=0))
        put(7, acc_a[: 2 * R, :R])
        put(8, jnp.concatenate([acc_b[:, R:], acc_d[...]], axis=0))
        put(9, jnp.concatenate([acc_a[2 * R :, :R], acc_b[:, :R]], axis=0))


def project(rhs, bases):
    width = rhs.shape[1] // STEPS
    return pl.pallas_call(
        project_kernel,
        grid=(STEPS,),
        in_specs=[
            pl.BlockSpec((256, width), lambda i: (0, i)),
            pl.BlockSpec((5, R, width), lambda i: (0, 0, i)),
        ],
        out_specs=pl.BlockSpec((16, 10 * ROWS, R), lambda i: (0, 0, 0)),
        out_shape=jax.ShapeDtypeStruct((16, 10 * ROWS, R), BF16),
        scratch_shapes=[
            pltpu.VMEM((256, 5 * R), F32),
            pltpu.VMEM((3 * R, 2 * R), F32),
            pltpu.VMEM((R, 2 * R), F32),
            pltpu.VMEM((R, R), F32),
            pltpu.VMEM((R, R), F32),
        ],
        compiler_params=pltpu.CompilerParams(vmem_limit_bytes=VMEM_LIMIT),
    )(rhs, bases)


def local_call(kernel, place, shape, *arrays):
    whole = pl.BlockSpec(memory_space=pltpu.VMEM)
    return pl.pallas_call(
        kernel,
        in_specs=[pl.BlockSpec(memory_space=pltpu.SMEM)] + [whole] * len(arrays),
        out_specs=whole,
        out_shape=jax.ShapeDtypeStruct(shape, BF16),
        compiler_params=pltpu.CompilerParams(vmem_limit_bytes=VMEM_LIMIT),
    )(place, *arrays)


def couple_kernel(place, parts, coupling, out):
    total = parts[0].astype(F32)
    for source in range(1, 16):
        total += parts[source].astype(F32)
    total = total.astype(BF16)
    proj, gram = total[: 5 * ROWS], total[5 * ROWS :]
    first = dot(gram[: 2 * ROWS], coupling[4, 0])
    second = dot(gram[2 * ROWS : 3 * ROWS], coupling[3, 0])
    third = dot(gram[3 * ROWS : 4 * ROWS], coupling[2, 0])
    last = gram[4 * ROWS :]
    fourth = jnp.where(place[3] < 8, dot(last, coupling[3, 0]), dot(last, coupling[1, 0]))
    mixed = [first[:ROWS], first[ROWS:], second, third, fourth]
    halves = [m[:, R * half : R * (half + 1)].astype(BF16) for m in mixed for half in (0, 1)]
    whole = jnp.concatenate([proj] + halves, axis=0)
    for copy in range(4):
        out[copy] = whole


def piece(ref, position, lead=()):
    return ref[lead + (slice(ROWS * position, ROWS * (position + 1)), slice(None))].astype(F32)


def plane_kernel(place, quarters, out):
    rows = slice(ROWS * 11, ROWS * 15)
    total = quarters[0, rows].astype(F32)
    for x in range(1, 4):
        total += quarters[x, rows].astype(F32)
    total = total.astype(BF16)
    for copy in range(8):
        out[copy] = total


def nodes_kernel(place, quarters, planes, own_planes, out):
    def put(position, value):
        count = value.shape[0] // ROWS
        out[ROWS * position : ROWS * (position + count)] = value.astype(BF16)

    def quarter(x, start, stop):
        return quarters[x, ROWS * start : ROWS * stop].astype(F32)

    def plane(z, start, stop):
        return planes[z, ROWS * start : ROWS * stop].astype(F32)

    for node in range(2):
        put(4 * node, quarter(2 * node, 5, 9) + quarter(2 * node + 1, 5, 9))
    put(8, quarter(0, 9, 11) + quarter(1, 9, 11) + quarter(2, 9, 11) + quarter(3, 9, 11))
    for node in range(4):
        put(10 + 2 * node, plane(2 * node, 0, 2) + plane(2 * node + 1, 0, 2))
    for node in range(2):
        summed = plane(4 * node, 2, 4) + plane(4 * node + 1, 2, 4)
        summed += plane(4 * node + 2, 2, 4) + plane(4 * node + 3, 2, 4)
        mine = own_planes[0, 2 * ROWS :].astype(F32)
        put(18 + 2 * node, jnp.where(place[3] < 8, mine, summed))


def gathered(ref, position):
    return ref[:, ROWS * position : ROWS * (position + 1), :].reshape(16 * ROWS, R)


def level43_kernel(place, quarters, mixed, coupling, out, keep):
    def proj(x, level):
        return quarters[x, ROWS * level : ROWS * (level + 1)]

    sums = []
    for node in range(2):
        left, right = proj(2 * node, 4), proj(2 * node + 1, 4)
        base = 4 * node
        updates = []
        for part in range(2):
            both = dot_t(left, gathered(mixed, base + 2 * part)) + dot_t(right, gathered(mixed, base + 2 * part + 1))
            updates += [both[:, :R], both[:, R:]]
        sums.append(
            [
                proj(2 * node, l).astype(F32) + proj(2 * node + 1, l).astype(F32) - updates[l]
                for l in range(4)
            ]
        )
    left, right = sums[0][3].astype(BF16), sums[1][3].astype(BF16)
    both = dot_t(left, gathered(mixed, 8)) + dot_t(right, gathered(mixed, 9))
    last = dot_t(left, gathered(mixed, 18)[:R]) + dot_t(right, gathered(mixed, 19)[:R])
    updates = [both[:, :R], both[:, R:], last]
    result = [(sums[0][l] + sums[1][l] - updates[l]).astype(BF16) for l in range(3)]
    result = jnp.concatenate(result, axis=0)
    for copy in range(8):
        out[copy] = result
    x = place[1]
    node = x // 2
    four = dot_t(proj(2 * node, 4), coupling[4, 0][:, :R]) + dot_t(proj(2 * node + 1, 4), coupling[4, 0][:, R:])
    three = dot_t(left, coupling[3, 0][:, :R]) + dot_t(right, coupling[3, 0][:, R:])
    keep[:ROWS] = four.astype(BF16)
    keep[ROWS:] = three.astype(BF16)


def level210_kernel(place, planes, mixed, coupling, keep, out):
    z = place[0]

    def proj(plane, level):
        return planes[plane, ROWS * level : ROWS * (level + 1)]

    def apart(left, right, level):
        return dot_t(left, coupling[level, 0][:, :R]) + dot_t(right, coupling[level, 0][:, R:])

    ones, zeros = [], []
    for node in range(4):
        left, right = proj(2 * node, 2), proj(2 * node + 1, 2)
        both = dot_t(left, gathered(mixed, 10 + 2 * node)) + dot_t(right, gathered(mixed, 11 + 2 * node))
        zeros.append(proj(2 * node, 0).astype(F32) + proj(2 * node + 1, 0).astype(F32) - both[:, :R])
        ones.append(proj(2 * node, 1).astype(F32) + proj(2 * node + 1, 1).astype(F32) - both[:, R:])
    ones = [value.astype(BF16) for value in ones]
    ends = []
    for node in range(2):
        left, right = ones[2 * node], ones[2 * node + 1]
        update = dot_t(left, gathered(mixed, 18 + 2 * node)[R:]) + dot_t(right, gathered(mixed, 19 + 2 * node)[R:])
        ends.append((zeros[2 * node] + zeros[2 * node + 1] - update).astype(BF16))
    pair = 2 * (z // 2)
    two = apart(proj(pair, 2), proj(pair + 1, 2), 2)
    one = jnp.where(z < 4, apart(ones[0], ones[1], 1), apart(ones[2], ones[3], 1))
    zero = apart(ends[0], ends[1], 0)
    out[: 3 * ROWS] = jnp.concatenate([zero, one, two], axis=0).astype(BF16)
    out[3 * ROWS : 4 * ROWS] = keep[ROWS:]
    out[4 * ROWS :] = keep[:ROWS]


def apply_kernel(rhs, bases, corr, out, lhs):
    @pl.when(pl.program_id(0) == 0)
    def _():
        for level in range(5):
            lhs[:, R * level : R * (level + 1)] = gathered(corr, level)

    update = dot(lhs[...], bases[...].reshape(5 * R, bases.shape[2]))
    out[...] = (rhs[...].astype(F32) - update).astype(BF16)


def apply_levels(rhs, bases, corr):
    width = rhs.shape[1] // STEPS
    return pl.pallas_call(
        apply_kernel,
        grid=(STEPS,),
        in_specs=[
            pl.BlockSpec((256, width), lambda i: (0, i)),
            pl.BlockSpec((5, R, width), lambda i: (0, 0, i)),
            pl.BlockSpec((16, 5 * ROWS, R), lambda i: (0, 0, 0)),
        ],
        out_specs=pl.BlockSpec((256, width), lambda i: (0, i)),
        out_shape=jax.ShapeDtypeStruct(rhs.shape, BF16),
        scratch_shapes=[pltpu.VMEM((256, 5 * R), BF16)],
        compiler_params=pltpu.CompilerParams(vmem_limit_bytes=VMEM_LIMIT),
    )(rhs, bases, corr)


def on_device(rhs, bases, coupling):
    group = ("y", "c")
    member = lax.axis_index("y") * 2 + lax.axis_index("c")
    place = jnp.stack([lax.axis_index("z"), lax.axis_index("x"), member * 0, member]).astype(jnp.int32)
    exchange = functools.partial(lax.all_to_all, split_axis=0, concat_axis=0)

    parts = exchange(project(rhs, bases), group)
    quarters = local_call(couple_kernel, place, (4, 15 * ROWS, R), parts, coupling)
    quarters = exchange(quarters, "x")
    own_planes = local_call(plane_kernel, place, (8, 4 * ROWS, R), quarters)
    planes = exchange(own_planes, "z")
    mixed = local_call(nodes_kernel, place, (22 * ROWS, R), quarters, planes, own_planes)
    mixed = lax.all_gather(mixed, group)
    whole = pl.BlockSpec(memory_space=pltpu.VMEM)
    sums, keep = pl.pallas_call(
        level43_kernel,
        in_specs=[pl.BlockSpec(memory_space=pltpu.SMEM)] + [whole] * 3,
        out_specs=[whole, whole],
        out_shape=[
            jax.ShapeDtypeStruct((8, 3 * ROWS, R), BF16),
            jax.ShapeDtypeStruct((2 * ROWS, R), BF16),
        ],
        compiler_params=pltpu.CompilerParams(vmem_limit_bytes=VMEM_LIMIT),
    )(place, quarters, mixed, coupling)
    sums = exchange(sums, "z")
    corr = local_call(level210_kernel, place, (5 * ROWS, R), sums, mixed, coupling, keep)
    corr = lax.all_gather(corr, group)
    return apply_levels(rhs, bases, corr)


def solution(mesh):
    names = ("z", "x", "y", "c")
    split = Mesh(mesh.devices.reshape(8, 4, 8, 2), names)
    return jax.shard_map(
        on_device,
        mesh=split,
        in_specs=(P(None, names), P(None, None, names), P(None, names, None, None)),
        out_specs=P(None, names),
        check_vma=False,
    )
```

```python
import functools

import jax
import jax.numpy as jnp
from jax import lax
from jax.experimental import pallas as pl
from jax.experimental.pallas import tpu as pltpu
from jax.sharding import Mesh
from jax.sharding import PartitionSpec as P


ROWS = 16
PIECES = 5
R = 128
STEPS = 4
F32 = jnp.float32
BF16 = jnp.bfloat16
VMEM_LIMIT = 40 * 1024 * 1024


def dot_t(a, b):
    return lax.dot_general(a, b, (((1,), (1,)), ((), ())), preferred_element_type=F32)


def dot(a, b):
    return jnp.dot(a, b, preferred_element_type=F32)


def project_kernel(rhs, bases, out, acc_p, acc_a, acc_b, acc_c, acc_d):
    step = pl.program_id(0)

    @pl.when(step == 0)
    def _():
        for acc in (acc_p, acc_a, acc_b, acc_c, acc_d):
            acc[...] = jnp.zeros_like(acc)

    width = rhs.shape[1]
    everything = bases[...].reshape(5 * R, width)
    acc_p[...] += dot_t(rhs[...], everything)
    acc_a[...] += dot_t(everything[: 3 * R], everything[3 * R :])
    acc_b[...] += dot_t(everything[:R], everything[R : 3 * R])
    acc_c[...] += dot_t(everything[3 * R : 4 * R], everything[4 * R :])
    acc_d[...] += dot_t(everything[R : 2 * R], everything[2 * R : 3 * R])

    @pl.when(step == STEPS - 1)
    def _():
        def put(position, value):
            out[:, ROWS * position : ROWS * (position + 1), :] = value.astype(BF16).reshape(16, ROWS, R)

        for level in range(5):
            put(level, acc_p[:, R * level : R * (level + 1)])
        put(5, acc_a[: 2 * R, R:])
        put(6, jnp.concatenate([acc_a[2 * R :, R:], acc_c[...]], axis=0))
        put(7, acc_a[: 2 * R, :R])
        put(8, jnp.concatenate([acc_b[:, R:], acc_d[...]], axis=0))
        put(9, jnp.concatenate([acc_a[2 * R :, :R], acc_b[:, :R]], axis=0))


def project(rhs, bases):
    width = rhs.shape[1] // STEPS
    return pl.pallas_call(
        project_kernel,
        grid=(STEPS,),
        in_specs=[
            pl.BlockSpec((256, width), lambda i: (0, i)),
            pl.BlockSpec((5, R, width), lambda i: (0, 0, i)),
        ],
        out_specs=pl.BlockSpec((16, 10 * ROWS, R), lambda i: (0, 0, 0)),
        out_shape=jax.ShapeDtypeStruct((16, 10 * ROWS, R), BF16),
        scratch_shapes=[
            pltpu.VMEM((256, 5 * R), F32),
            pltpu.VMEM((3 * R, 2 * R), F32),
            pltpu.VMEM((R, 2 * R), F32),
            pltpu.VMEM((R, R), F32),
            pltpu.VMEM((R, R), F32),
        ],
        compiler_params=pltpu.CompilerParams(vmem_limit_bytes=VMEM_LIMIT),
    )(rhs, bases)


def local_call(kernel, place, shapes, *arrays):
    whole = pl.BlockSpec(memory_space=pltpu.VMEM)
    return pl.pallas_call(
        kernel,
        in_specs=[pl.BlockSpec(memory_space=pltpu.SMEM)] + [whole] * len(arrays),
        out_specs=[whole] * len(shapes),
        out_shape=[jax.ShapeDtypeStruct(shape, dtype) for shape, dtype in shapes],
        compiler_params=pltpu.CompilerParams(vmem_limit_bytes=VMEM_LIMIT),
    )(place, *arrays)


def couple_kernel(place, parts, coupling, out):
    total = parts[0].astype(F32)
    for source in range(1, 16):
        total += parts[source].astype(F32)
    total = total.astype(BF16)
    proj, gram = total[: 5 * ROWS], total[5 * ROWS :]
    first = dot(gram[: 2 * ROWS], coupling[4, 0])
    second = dot(gram[2 * ROWS : 3 * ROWS], coupling[3, 0])
    third = dot(gram[3 * ROWS : 4 * ROWS], coupling[2, 0])
    last = gram[4 * ROWS :]
    fourth = jnp.where(place[3] < 8, dot(last, coupling[3, 0]), dot(last, coupling[1, 0]))
    mixed = [first[:ROWS], first[ROWS:], second, third, fourth]
    halves = [m[:, R * half : R * (half + 1)].astype(BF16) for m in mixed for half in (0, 1)]
    whole = jnp.concatenate([proj] + halves, axis=0)
    for copy in range(4):
        out[copy] = whole


def nodes_kernel(place, quarters, out):
    def put(position, value):
        count = value.shape[0] // ROWS
        out[ROWS * position : ROWS * (position + count)] = value.astype(BF16)

    def quarter(x, start, stop):
        return quarters[x, ROWS * start : ROWS * stop].astype(F32)

    for node in range(2):
        put(4 * node, quarter(2 * node, 5, 9) + quarter(2 * node + 1, 5, 9))
    put(8, quarter(0, 9, 15) + quarter(1, 9, 15) + quarter(2, 9, 15) + quarter(3, 9, 15))


def gathered(ref, position):
    return ref[:, ROWS * position : ROWS * (position + 1), :].reshape(16 * ROWS, R)


def apart(left, right, coupling, level):
    return dot_t(left, coupling[level, 0][:, :R]) + dot_t(right, coupling[level, 0][:, R:])


def level43_kernel(place, quarters, mixed, coupling, two, rest, keep):
    def proj(x, level):
        return quarters[x, ROWS * level : ROWS * (level + 1)]

    sums = []
    for node in range(2):
        left, right = proj(2 * node, 4), proj(2 * node + 1, 4)
        base = 4 * node
        updates = []
        for part in range(2):
            both = dot_t(left, gathered(mixed, base + 2 * part)) + dot_t(right, gathered(mixed, base + 2 * part + 1))
            updates += [both[:, :R], both[:, R:]]
        sums.append(
            [
                proj(2 * node, l).astype(F32) + proj(2 * node + 1, l).astype(F32) - updates[l]
                for l in range(4)
            ]
        )
    left, right = sums[0][3].astype(BF16), sums[1][3].astype(BF16)
    both = dot_t(left, gathered(mixed, 8)) + dot_t(right, gathered(mixed, 9))
    last = dot_t(left, gathered(mixed, 12)[:R]) + dot_t(right, gathered(mixed, 13)[:R])
    two[...] = (sums[0][2] + sums[1][2] - last).astype(BF16)
    rest[:ROWS] = sums[0][1] + sums[1][1] - both[:, R:]
    rest[ROWS:] = sums[0][0] + sums[1][0] - both[:, :R]
    node = place[1] // 2
    four = apart(proj(2 * node, 4), proj(2 * node + 1, 4), coupling, 4)
    keep[:ROWS] = four.astype(BF16)
    keep[ROWS:] = apart(left, right, coupling, 3).astype(BF16)


def level2_kernel(place, mine, other, rest, mixed, coupling, one, zero, corr):
    first = place[0] % 2 == 0
    left = jnp.where(first, mine[...], other[...])
    right = jnp.where(first, other[...], mine[...])
    both = dot_t(left, gathered(mixed, 10)) + dot_t(right, gathered(mixed, 11))
    value = (rest[:ROWS] - both[:, R:]).astype(BF16)
    for copy in range(4):
        one[copy] = value
    zero[...] = rest[ROWS:] - both[:, :R]
    corr[...] = apart(left, right, coupling, 2).astype(BF16)


def level1_kernel(place, ones, rest, mixed, coupling, zero, corr):
    ones = [ones[plane].astype(F32) for plane in range(4)]
    left, right = (ones[0] + ones[1]).astype(BF16), (ones[2] + ones[3]).astype(BF16)
    update = dot_t(left, gathered(mixed, 12)[R:]) + dot_t(right, gathered(mixed, 13)[R:])
    value = (rest[...] - update).astype(BF16)
    for copy in range(8):
        zero[copy] = value
    corr[...] = apart(left, right, coupling, 1).astype(BF16)


def level0_kernel(place, zeros, coupling, keep, two, one, out):
    zeros = [zeros[plane].astype(F32) for plane in range(8)]
    left, right = sum(zeros[1:4], zeros[0]).astype(BF16), sum(zeros[5:], zeros[4]).astype(BF16)
    out[:ROWS] = apart(left, right, coupling, 0).astype(BF16)
    out[ROWS : 2 * ROWS] = one[...]
    out[2 * ROWS : 3 * ROWS] = two[...]
    out[3 * ROWS : 4 * ROWS] = keep[ROWS:]
    out[4 * ROWS :] = keep[:ROWS]


def apply_kernel(rhs, bases, corr, out, lhs):
    @pl.when(pl.program_id(0) == 0)
    def _():
        for level in range(5):
            lhs[:, R * level : R * (level + 1)] = gathered(corr, level)

    update = dot(lhs[...], bases[...].reshape(5 * R, bases.shape[2]))
    out[...] = (rhs[...].astype(F32) - update).astype(BF16)


def apply_levels(rhs, bases, corr):
    width = rhs.shape[1] // STEPS
    return pl.pallas_call(
        apply_kernel,
        grid=(STEPS,),
        in_specs=[
            pl.BlockSpec((256, width), lambda i: (0, i)),
            pl.BlockSpec((5, R, width), lambda i: (0, 0, i)),
            pl.BlockSpec((16, 5 * ROWS, R), lambda i: (0, 0, 0)),
        ],
        out_specs=pl.BlockSpec((256, width), lambda i: (0, i)),
        out_shape=jax.ShapeDtypeStruct(rhs.shape, BF16),
        scratch_shapes=[pltpu.VMEM((256, 5 * R), BF16)],
        compiler_params=pltpu.CompilerParams(vmem_limit_bytes=VMEM_LIMIT),
    )(rhs, bases, corr)


def on_device(rhs, bases, coupling):
    group = ("y", "c")
    member = lax.axis_index("y") * 2 + lax.axis_index("c")
    z = lax.axis_index("zh") * 4 + lax.axis_index("zl")
    place = jnp.stack([z, lax.axis_index("x"), member * 0, member]).astype(jnp.int32)
    exchange = functools.partial(lax.all_to_all, split_axis=0, concat_axis=0)
    block = (ROWS, R)

    parts = exchange(project(rhs, bases), group)
    (quarters,) = local_call(couple_kernel, place, [((4, 15 * ROWS, R), BF16)], parts, coupling)
    quarters = exchange(quarters, "x")
    (mixed,) = local_call(nodes_kernel, place, [((14 * ROWS, R), BF16)], quarters)
    mixed = lax.all_gather(mixed, group)
    two, rest, keep = local_call(
        level43_kernel,
        place,
        [(block, BF16), ((2 * ROWS, R), F32), ((2 * ROWS, R), BF16)],
        quarters,
        mixed,
        coupling,
    )
    other = lax.ppermute(two, "zl", [(plane, plane ^ 1) for plane in range(4)])
    ones, rest, corr_2 = local_call(
        level2_kernel,
        place,
        [((4, *block), BF16), (block, F32), (block, BF16)],
        two,
        other,
        rest,
        mixed,
        coupling,
    )
    ones = exchange(ones, "zl")
    zeros, corr_1 = local_call(
        level1_kernel, place, [((8, *block), BF16), (block, BF16)], ones, rest, mixed, coupling
    )
    zeros = exchange(zeros, ("zh", "zl"))
    (corr,) = local_call(
        level0_kernel, place, [((5 * ROWS, R), BF16)], zeros, coupling, keep, corr_2, corr_1
    )
    corr = lax.all_gather(corr, group)
    return apply_levels(rhs, bases, corr)


def solution(mesh):
    names = ("zh", "zl", "x", "y", "c")
    split = Mesh(mesh.devices.reshape(2, 4, 4, 8, 2), names)
    return jax.shard_map(
        on_device,
        mesh=split,
        in_specs=(P(None, names), P(None, None, names), P(None, names, None, None)),
        out_specs=P(None, names),
        check_vma=False,
    )
```

```python
import functools

import jax
import jax.numpy as jnp
from jax import lax
from jax.experimental import pallas as pl
from jax.experimental.pallas import tpu as pltpu
from jax.sharding import Mesh
from jax.sharding import PartitionSpec as P


ROWS = 16
R = 128
CHUNKS = 2
OUT_CHUNKS = 4
HALF = 8
F32 = jnp.float32
BF16 = jnp.bfloat16
VMEM_LIMIT = 40 * 1024 * 1024
PROJECT_VMEM_LIMIT = 53 * 1024 * 1024


def dot_t(a, b):
    return lax.dot_general(a, b, (((1,), (1,)), ((), ())), preferred_element_type=F32)


def dot(a, b):
    return jnp.dot(a, b, preferred_element_type=F32)


def project_kernel(rhs, bases, mine, other, stack, high, middle, low, sems):
    width = rhs.shape[1] // CHUNKS
    copies = []
    for chunk in range(CHUNKS):
        columns = pl.ds(chunk * width, width)
        copies.append([pltpu.make_async_copy(rhs.at[:, columns], stack.at[: 2 * R, columns], sems.at[0, chunk])])
        for level in range(5):
            rows = pl.ds((2 + level) * R, R)
            copies[chunk].append(
                pltpu.make_async_copy(
                    bases.at[level, :, columns], stack.at[rows, columns], sems.at[level + 1, chunk]
                )
            )
        for copy in copies[chunk]:
            copy.start()

    def add(acc, chunk, value):
        if chunk == 0:
            acc[...] = value
        else:
            acc[...] += value

    for chunk in range(CHUNKS):
        columns = slice(chunk * width, (chunk + 1) * width)
        for copy in copies[chunk]:
            copy.wait()
        add(high, chunk, dot_t(stack[: 6 * R, columns], stack[5 * R :, columns]))
        add(middle, chunk, dot_t(stack[: 4 * R, columns], stack[3 * R : 5 * R, columns]))
        add(low, chunk, dot_t(stack[: 2 * R, columns], stack[2 * R : 3 * R, columns]))

    def tile(ref, row, column):
        return ref[row * R : (row + 1) * R, column * R : (column + 1) * R]

    first = lax.axis_index("c") == 0

    def put(position, zero, one):
        rows = slice(ROWS * position, ROWS * (position + 1))
        zero, one = zero.astype(BF16), one.astype(BF16)
        mine[:, rows, :] = jnp.where(first, zero, one).reshape(HALF, ROWS, R)
        other[:, rows, :] = jnp.where(first, one, zero).reshape(HALF, ROWS, R)

    for level, (ref, column) in enumerate([(low, 0), (middle, 0), (middle, 1), (high, 0), (high, 1)]):
        put(level, tile(ref, 0, column), tile(ref, 1, column))
    put(5, tile(high, 2, 1), tile(high, 3, 1))
    put(6, tile(high, 4, 1), tile(high, 5, 1))
    put(7, tile(high, 2, 0), tile(high, 3, 0))
    put(8, tile(middle, 2, 1), tile(middle, 3, 1))
    put(9, tile(high, 4, 0), tile(middle, 2, 0))


def project(rhs, bases):
    hbm = pl.BlockSpec(memory_space=pltpu.HBM)
    whole = pl.BlockSpec(memory_space=pltpu.VMEM)
    return pl.pallas_call(
        project_kernel,
        in_specs=[hbm, hbm],
        out_specs=[whole, whole],
        out_shape=[jax.ShapeDtypeStruct((HALF, 10 * ROWS, R), BF16)] * 2,
        scratch_shapes=[
            pltpu.VMEM((7 * R, rhs.shape[1]), BF16),
            pltpu.VMEM((6 * R, 2 * R), F32),
            pltpu.VMEM((4 * R, 2 * R), F32),
            pltpu.VMEM((2 * R, R), F32),
            pltpu.SemaphoreType.DMA((6, CHUNKS)),
        ],
        compiler_params=pltpu.CompilerParams(vmem_limit_bytes=PROJECT_VMEM_LIMIT),
    )(rhs, bases)


def local_call(kernel, shapes, *arrays):
    whole = pl.BlockSpec(memory_space=pltpu.VMEM)
    return pl.pallas_call(
        kernel,
        in_specs=[whole] * len(arrays),
        out_specs=[whole] * len(shapes),
        out_shape=[jax.ShapeDtypeStruct(shape, dtype) for shape, dtype in shapes],
        compiler_params=pltpu.CompilerParams(vmem_limit_bytes=VMEM_LIMIT),
    )(*arrays)


def chip_kernel(mine, theirs, out):
    out[...] = (mine[...].astype(F32) + theirs[...].astype(F32)).astype(BF16)


def couple_kernel(parts, coupling, out):
    total = parts[0].astype(F32)
    for source in range(1, HALF):
        total += parts[source].astype(F32)
    total = total.astype(BF16)
    proj, gram = total[: 5 * ROWS], total[5 * ROWS :]
    first = dot(gram[: 2 * ROWS], coupling[4, 0])
    second = dot(gram[2 * ROWS : 3 * ROWS], coupling[3, 0])
    third = dot(gram[3 * ROWS : 4 * ROWS], coupling[2, 0])
    last = gram[4 * ROWS :]
    fourth = jnp.where(lax.axis_index("c") == 0, dot(last, coupling[3, 0]), dot(last, coupling[1, 0]))
    mixed = [first[:ROWS], first[ROWS:], second, third, fourth]
    halves = [m[:, R * half : R * (half + 1)].astype(BF16) for m in mixed for half in (0, 1)]
    whole = jnp.concatenate([proj] + halves, axis=0)
    for copy in range(4):
        out[copy] = whole


def nodes_kernel(quarters, out):
    def put(position, value):
        count = value.shape[0] // ROWS
        out[ROWS * position : ROWS * (position + count)] = value.astype(BF16)

    def quarter(x, start, stop):
        return quarters[x, ROWS * start : ROWS * stop].astype(F32)

    for node in range(2):
        put(4 * node, quarter(2 * node, 5, 9) + quarter(2 * node + 1, 5, 9))
    put(8, quarter(0, 9, 15) + quarter(1, 9, 15) + quarter(2, 9, 15) + quarter(3, 9, 15))


def gathered(ref, position):
    rows = slice(ROWS * position, ROWS * (position + 1))
    return jnp.concatenate([ref[2 * y + c, rows] for c in range(2) for y in range(HALF)], axis=0)


def apart(left, right, coupling, level):
    return dot_t(left, coupling[level, 0][:, :R]) + dot_t(right, coupling[level, 0][:, R:])


def level43_kernel(quarters, mixed, coupling, two, rest, keep):
    def proj(x, level):
        return quarters[x, ROWS * level : ROWS * (level + 1)]

    sums = []
    for node in range(2):
        left, right = proj(2 * node, 4), proj(2 * node + 1, 4)
        base = 4 * node
        updates = []
        for part in range(2):
            both = dot_t(left, gathered(mixed, base + 2 * part)) + dot_t(right, gathered(mixed, base + 2 * part + 1))
            updates += [both[:, :R], both[:, R:]]
        sums.append(
            [
                proj(2 * node, l).astype(F32) + proj(2 * node + 1, l).astype(F32) - updates[l]
                for l in range(4)
            ]
        )
    left, right = sums[0][3].astype(BF16), sums[1][3].astype(BF16)
    both = dot_t(left, gathered(mixed, 8)) + dot_t(right, gathered(mixed, 9))
    last = dot_t(left, gathered(mixed, 12)[:R]) + dot_t(right, gathered(mixed, 13)[:R])
    two[...] = (sums[0][2] + sums[1][2] - last).astype(BF16)
    rest[:ROWS] = sums[0][1] + sums[1][1] - both[:, R:]
    rest[ROWS:] = sums[0][0] + sums[1][0] - both[:, :R]
    node = lax.axis_index("x") // 2
    four = apart(proj(2 * node, 4), proj(2 * node + 1, 4), coupling, 4)
    keep[:ROWS] = four.astype(BF16)
    keep[ROWS:] = apart(left, right, coupling, 3).astype(BF16)


def level2_kernel(mine, other, rest, mixed, coupling, one, zero, corr):
    first = lax.axis_index("zl") % 2 == 0
    left = jnp.where(first, mine[...], other[...])
    right = jnp.where(first, other[...], mine[...])
    both = dot_t(left, gathered(mixed, 10)) + dot_t(right, gathered(mixed, 11))
    value = (rest[:ROWS] - both[:, R:]).astype(BF16)
    for copy in range(4):
        one[copy] = value
    zero[...] = rest[ROWS:] - both[:, :R]
    corr[...] = apart(left, right, coupling, 2).astype(BF16)


def level1_kernel(ones, rest, mixed, coupling, zero, corr):
    ones = [ones[plane].astype(F32) for plane in range(4)]
    left, right = (ones[0] + ones[1]).astype(BF16), (ones[2] + ones[3]).astype(BF16)
    update = dot_t(left, gathered(mixed, 12)[R:]) + dot_t(right, gathered(mixed, 13)[R:])
    value = (rest[...] - update).astype(BF16)
    for copy in range(8):
        zero[copy] = value
    corr[...] = apart(left, right, coupling, 1).astype(BF16)


def level0_kernel(zeros, coupling, keep, two, one, out):
    zeros = [zeros[plane].astype(F32) for plane in range(8)]
    left, right = sum(zeros[1:4], zeros[0]).astype(BF16), sum(zeros[5:], zeros[4]).astype(BF16)
    out[:ROWS] = apart(left, right, coupling, 0).astype(BF16)
    out[ROWS : 2 * ROWS] = one[...]
    out[2 * ROWS : 3 * ROWS] = two[...]
    out[3 * ROWS : 4 * ROWS] = keep[ROWS:]
    out[4 * ROWS :] = keep[:ROWS]


def apply_kernel(rhs, bases, corr, out, here, sems):
    everything = jnp.concatenate([gathered(corr, level) for level in range(5)], axis=1)
    width = rhs.shape[1] // OUT_CHUNKS
    copies = []
    for chunk in range(OUT_CHUNKS):
        columns = slice(chunk * width, (chunk + 1) * width)
        update = dot(everything, bases[:, :, columns].reshape(5 * R, width))
        here[:, columns] = (rhs[:, columns].astype(F32) - update).astype(BF16)
        columns = pl.ds(chunk * width, width)
        copies.append(pltpu.make_async_copy(here.at[:, columns], out.at[:, columns], sems.at[chunk]))
        copies[-1].start()
    for copy in copies:
        copy.wait()


def apply_levels(rhs, bases, corr):
    whole = pl.BlockSpec(memory_space=pltpu.VMEM)
    return pl.pallas_call(
        apply_kernel,
        in_specs=[whole, whole, whole],
        out_specs=pl.BlockSpec(memory_space=pltpu.HBM),
        out_shape=jax.ShapeDtypeStruct(rhs.shape, BF16),
        scratch_shapes=[pltpu.VMEM(rhs.shape, BF16), pltpu.SemaphoreType.DMA((OUT_CHUNKS,))],
        compiler_params=pltpu.CompilerParams(vmem_limit_bytes=VMEM_LIMIT),
    )(rhs, bases, corr)


def on_device(rhs, bases, coupling):
    group = ("y", "c")
    exchange = functools.partial(lax.all_to_all, split_axis=0, concat_axis=0)
    block = (ROWS, R)

    mine, other = project(rhs, bases)
    theirs = lax.ppermute(other, "c", [(0, 1), (1, 0)])
    (parts,) = local_call(chip_kernel, [(mine.shape, BF16)], mine, theirs)
    parts = exchange(parts, "y")
    (quarters,) = local_call(couple_kernel, [((4, 15 * ROWS, R), BF16)], parts, coupling)
    quarters = exchange(quarters, "x")
    (mixed,) = local_call(nodes_kernel, [((14 * ROWS, R), BF16)], quarters)
    mixed = lax.all_gather(mixed, group)
    two, rest, keep = local_call(
        level43_kernel,
        [(block, BF16), ((2 * ROWS, R), F32), ((2 * ROWS, R), BF16)],
        quarters,
        mixed,
        coupling,
    )
    other = lax.ppermute(two, "zl", [(plane, plane ^ 1) for plane in range(4)])
    ones, rest, corr_2 = local_call(
        level2_kernel,
        [((4, *block), BF16), (block, F32), (block, BF16)],
        two,
        other,
        rest,
        mixed,
        coupling,
    )
    ones = exchange(ones, "zl")
    zeros, corr_1 = local_call(
        level1_kernel, [((8, *block), BF16), (block, BF16)], ones, rest, mixed, coupling
    )
    zeros = exchange(zeros, ("zh", "zl"))
    (corr,) = local_call(
        level0_kernel, [((5 * ROWS, R), BF16)], zeros, coupling, keep, corr_2, corr_1
    )
    corr = lax.all_gather(corr, group)
    return apply_levels(rhs, bases, corr)


def solution(mesh):
    names = ("zh", "zl", "x", "y", "c")
    split = Mesh(mesh.devices.reshape(2, 4, 4, 8, 2), names)
    return jax.shard_map(
        on_device,
        mesh=split,
        in_specs=(P(None, names), P(None, None, names), P(None, names, None, None)),
        out_specs=P(None, names),
        check_vma=False,
    )
```

```python
import functools

import jax
import jax.numpy as jnp
from jax import lax
from jax.experimental import pallas as pl
from jax.experimental.pallas import tpu as pltpu
from jax.sharding import Mesh
from jax.sharding import PartitionSpec as P


ROWS = 16
R = 128
CHUNKS = 2
OUT_CHUNKS = 4
HALF = 8
F32 = jnp.float32
BF16 = jnp.bfloat16
VMEM_LIMIT = 40 * 1024 * 1024
PROJECT_VMEM_LIMIT = 53 * 1024 * 1024


def dot_t(a, b):
    return lax.dot_general(a, b, (((1,), (1,)), ((), ())), preferred_element_type=F32)


def dot(a, b):
    return jnp.dot(a, b, preferred_element_type=F32)


def project_kernel(rhs, bases, mine, other, stack, high, middle, low, sems):
    width = rhs.shape[1] // CHUNKS
    copies = []
    for chunk in range(CHUNKS):
        columns = pl.ds(chunk * width, width)
        copies.append([pltpu.make_async_copy(rhs.at[:, columns], stack.at[: 2 * R, columns], sems.at[0, chunk])])
        for level in range(5):
            rows = pl.ds((2 + level) * R, R)
            copies[chunk].append(
                pltpu.make_async_copy(
                    bases.at[level, :, columns], stack.at[rows, columns], sems.at[level + 1, chunk]
                )
            )
        for copy in copies[chunk]:
            copy.start()

    def add(acc, chunk, value):
        if chunk == 0:
            acc[...] = value
        else:
            acc[...] += value

    for chunk in range(CHUNKS):
        columns = slice(chunk * width, (chunk + 1) * width)
        for copy in copies[chunk]:
            copy.wait()
        add(high, chunk, dot_t(stack[: 6 * R, columns], stack[5 * R :, columns]))
        add(middle, chunk, dot_t(stack[: 4 * R, columns], stack[3 * R : 5 * R, columns]))
        add(low, chunk, dot_t(stack[: 2 * R, columns], stack[2 * R : 3 * R, columns]))

    def tile(ref, row, column):
        return ref[row * R : (row + 1) * R, column * R : (column + 1) * R]

    first = lax.axis_index("c") == 0

    def put(position, zero, one):
        rows = slice(ROWS * position, ROWS * (position + 1))
        zero, one = zero.astype(BF16), one.astype(BF16)
        mine[:, rows, :] = jnp.where(first, zero, one).reshape(HALF, ROWS, R)
        other[:, rows, :] = jnp.where(first, one, zero).reshape(HALF, ROWS, R)

    for level, (ref, column) in enumerate([(low, 0), (middle, 0), (middle, 1), (high, 0), (high, 1)]):
        put(level, tile(ref, 0, column), tile(ref, 1, column))
    put(5, tile(high, 2, 1), tile(high, 3, 1))
    put(6, tile(high, 4, 1), tile(high, 5, 1))
    put(7, tile(high, 2, 0), tile(high, 3, 0))
    put(8, tile(middle, 2, 1), tile(middle, 3, 1))
    put(9, tile(high, 4, 0), tile(middle, 2, 0))


def project(rhs, bases):
    hbm = pl.BlockSpec(memory_space=pltpu.HBM)
    whole = pl.BlockSpec(memory_space=pltpu.VMEM)
    return pl.pallas_call(
        project_kernel,
        in_specs=[hbm, hbm],
        out_specs=[whole, whole],
        out_shape=[jax.ShapeDtypeStruct((HALF, 10 * ROWS, R), BF16)] * 2,
        scratch_shapes=[
            pltpu.VMEM((7 * R, rhs.shape[1]), BF16),
            pltpu.VMEM((6 * R, 2 * R), F32),
            pltpu.VMEM((4 * R, 2 * R), F32),
            pltpu.VMEM((2 * R, R), F32),
            pltpu.SemaphoreType.DMA((6, CHUNKS)),
        ],
        compiler_params=pltpu.CompilerParams(vmem_limit_bytes=PROJECT_VMEM_LIMIT),
    )(rhs, bases)


def local_call(kernel, shapes, *arrays):
    whole = pl.BlockSpec(memory_space=pltpu.VMEM)
    return pl.pallas_call(
        kernel,
        in_specs=[whole] * len(arrays),
        out_specs=[whole] * len(shapes),
        out_shape=[jax.ShapeDtypeStruct(shape, dtype) for shape, dtype in shapes],
        compiler_params=pltpu.CompilerParams(vmem_limit_bytes=VMEM_LIMIT),
    )(*arrays)


def chip_kernel(mine, theirs, out):
    out[...] = (mine[...].astype(F32) + theirs[...].astype(F32)).astype(BF16)


def couple_kernel(parts, coupling, out):
    total = parts[0].astype(F32)
    for source in range(1, HALF):
        total += parts[source].astype(F32)
    total = total.astype(BF16)
    proj, gram = total[: 5 * ROWS], total[5 * ROWS :]
    first = dot(gram[: 2 * ROWS], coupling[4, 0])
    second = dot(gram[2 * ROWS : 3 * ROWS], coupling[3, 0])
    third = dot(gram[3 * ROWS : 4 * ROWS], coupling[2, 0])
    last = gram[4 * ROWS :]
    fourth = jnp.where(lax.axis_index("c") == 0, dot(last, coupling[3, 0]), dot(last, coupling[1, 0]))
    mixed = [first[:ROWS], first[ROWS:], second, third, fourth]
    halves = [m[:, R * half : R * (half + 1)].astype(BF16) for m in mixed for half in (0, 1)]
    whole = jnp.concatenate([proj] + halves, axis=0)
    for copy in range(4):
        out[copy] = whole


def quarter_sum(quarters, start, stop):
    rows = slice(ROWS * start, ROWS * stop)
    return sum((quarters[x, rows].astype(F32) for x in range(1, 4)), quarters[0, rows].astype(F32))


def plane_kernel(quarters, out):
    total = quarter_sum(quarters, 11, 15).astype(BF16)
    for plane in range(4):
        second, first = plane % 2, 2 + plane // 2
        out[plane, :ROWS] = total[ROWS * second : ROWS * (second + 1)]
        out[plane, ROWS:] = total[ROWS * first : ROWS * (first + 1)]


def nodes_kernel(quarters, planes, out):
    def put(position, value):
        count = value.shape[0] // ROWS
        out[ROWS * position : ROWS * (position + count)] = value.astype(BF16)

    def quarter(x, start, stop):
        return quarters[x, ROWS * start : ROWS * stop].astype(F32)

    for node in range(2):
        put(4 * node, quarter(2 * node, 5, 9) + quarter(2 * node + 1, 5, 9))
    put(8, quarter_sum(quarters, 9, 11))
    summed = planes[0].astype(F32) + planes[1].astype(F32) + planes[2].astype(F32) + planes[3].astype(F32)
    last = quarter_sum(quarters, 13, 15)
    here = lax.axis_index("c") == 0
    put(10, jnp.where(here, last[:ROWS], summed[ROWS:]))
    put(11, last[ROWS:])
    pair = 2 * (lax.axis_index("zl") // 2)
    put(12, planes[pair, :ROWS].astype(F32) + planes[pair + 1, :ROWS].astype(F32))


def gathered(ref, position):
    rows = slice(ROWS * position, ROWS * (position + 1))
    return jnp.concatenate([ref[2 * y + c, rows] for c in range(2) for y in range(HALF)], axis=0)


def apart(left, right, coupling, level):
    return dot_t(left, coupling[level, 0][:, :R]) + dot_t(right, coupling[level, 0][:, R:])


def levels_kernel(quarters, mixed, coupling, out, keep):
    def proj(x, level):
        return quarters[x, ROWS * level : ROWS * (level + 1)]

    sums = []
    for node in range(2):
        left, right = proj(2 * node, 4), proj(2 * node + 1, 4)
        base = 4 * node
        updates = []
        for part in range(2):
            both = dot_t(left, gathered(mixed, base + 2 * part)) + dot_t(right, gathered(mixed, base + 2 * part + 1))
            updates += [both[:, :R], both[:, R:]]
        sums.append(
            [
                proj(2 * node, l).astype(F32) + proj(2 * node + 1, l).astype(F32) - updates[l]
                for l in range(4)
            ]
        )
    left, right = sums[0][3].astype(BF16), sums[1][3].astype(BF16)
    both = dot_t(left, gathered(mixed, 8)) + dot_t(right, gathered(mixed, 9))
    last = gathered(mixed, 10)
    update = dot_t(left, last[:R]) + dot_t(right, gathered(mixed, 11)[:R])
    two = (sums[0][2] + sums[1][2] - update).astype(BF16)
    lower = dot_t(two, gathered(mixed, 12))
    one = (sums[0][1] + sums[1][1] - both[:, R:] - lower[:, R:]).astype(BF16)
    zero = sums[0][0] + sums[1][0] - both[:, :R] - lower[:, :R] - dot_t(one, last[R:])
    result = jnp.concatenate([zero.astype(BF16), one, two], axis=0)
    for copy in range(8):
        out[copy] = result
    node = lax.axis_index("x") // 2
    four = apart(proj(2 * node, 4), proj(2 * node + 1, 4), coupling, 4)
    keep[:ROWS] = four.astype(BF16)
    keep[ROWS:] = apart(left, right, coupling, 3).astype(BF16)


def corr_kernel(planes, coupling, keep, out):
    def proj(plane, level):
        return planes[plane, ROWS * level : ROWS * (level + 1)]

    def over(level, first, count):
        return sum(
            (proj(first + plane, level).astype(F32) for plane in range(1, count)), proj(first, level).astype(F32)
        ).astype(BF16)

    z = lax.axis_index("zh") * 4 + lax.axis_index("zl")
    pair, quad = 2 * (z // 2), 4 * (z // 4)
    out[:ROWS] = apart(over(0, 0, 4), over(0, 4, 4), coupling, 0).astype(BF16)
    out[ROWS : 2 * ROWS] = apart(over(1, quad, 2), over(1, quad + 2, 2), coupling, 1).astype(BF16)
    out[2 * ROWS : 3 * ROWS] = apart(proj(pair, 2), proj(pair + 1, 2), coupling, 2).astype(BF16)
    out[3 * ROWS : 4 * ROWS] = keep[ROWS:]
    out[4 * ROWS :] = keep[:ROWS]


def apply_kernel(rhs, bases, corr, out, here, sems):
    everything = jnp.concatenate([gathered(corr, level) for level in range(5)], axis=1)
    width = rhs.shape[1] // OUT_CHUNKS
    copies = []
    for chunk in range(OUT_CHUNKS):
        columns = slice(chunk * width, (chunk + 1) * width)
        update = dot(everything, bases[:, :, columns].reshape(5 * R, width))
        here[:, columns] = (rhs[:, columns].astype(F32) - update).astype(BF16)
        columns = pl.ds(chunk * width, width)
        copies.append(pltpu.make_async_copy(here.at[:, columns], out.at[:, columns], sems.at[chunk]))
        copies[-1].start()
    for copy in copies:
        copy.wait()


def apply_levels(rhs, bases, corr):
    whole = pl.BlockSpec(memory_space=pltpu.VMEM)
    return pl.pallas_call(
        apply_kernel,
        in_specs=[whole, whole, whole],
        out_specs=pl.BlockSpec(memory_space=pltpu.HBM),
        out_shape=jax.ShapeDtypeStruct(rhs.shape, BF16),
        scratch_shapes=[pltpu.VMEM(rhs.shape, BF16), pltpu.SemaphoreType.DMA((OUT_CHUNKS,))],
        compiler_params=pltpu.CompilerParams(vmem_limit_bytes=VMEM_LIMIT),
    )(rhs, bases, corr)


def on_device(rhs, bases, coupling):
    group = ("y", "c")
    exchange = functools.partial(lax.all_to_all, split_axis=0, concat_axis=0)

    mine, other = project(rhs, bases)
    theirs = lax.ppermute(other, "c", [(0, 1), (1, 0)])
    (parts,) = local_call(chip_kernel, [(mine.shape, BF16)], mine, theirs)
    parts = exchange(parts, "y")
    (quarters,) = local_call(couple_kernel, [((4, 15 * ROWS, R), BF16)], parts, coupling)
    quarters = exchange(quarters, "x")
    (planes,) = local_call(plane_kernel, [((4, 2 * ROWS, R), BF16)], quarters)
    planes = exchange(planes, "zl")
    (mixed,) = local_call(nodes_kernel, [((13 * ROWS, R), BF16)], quarters, planes)
    mixed = lax.all_gather(mixed, group)
    lower, keep = local_call(
        levels_kernel,
        [((8, 3 * ROWS, R), BF16), ((2 * ROWS, R), BF16)],
        quarters,
        mixed,
        coupling,
    )
    lower = exchange(lower, ("zh", "zl"))
    (corr,) = local_call(corr_kernel, [((5 * ROWS, R), BF16)], lower, coupling, keep)
    corr = lax.all_gather(corr, group)
    return apply_levels(rhs, bases, corr)


def solution(mesh):
    names = ("zh", "zl", "x", "y", "c")
    split = Mesh(mesh.devices.reshape(2, 4, 4, 8, 2), names)
    return jax.shard_map(
        on_device,
        mesh=split,
        in_specs=(P(None, names), P(None, None, names), P(None, names, None, None)),
        out_specs=P(None, names),
        check_vma=False,
    )
```

```python
import functools

import jax
import jax.numpy as jnp
from jax import lax
from jax.experimental import pallas as pl
from jax.experimental.pallas import tpu as pltpu
from jax.sharding import Mesh
from jax.sharding import PartitionSpec as P


ROWS = 16
R = 128
CHUNKS = 2
OUT_CHUNKS = 2
HALF = 8
F32 = jnp.float32
BF16 = jnp.bfloat16
VMEM_LIMIT = 40 * 1024 * 1024
PROJECT_VMEM_LIMIT = 53 * 1024 * 1024


def dot_t(a, b):
    return lax.dot_general(a, b, (((1,), (1,)), ((), ())), preferred_element_type=F32)


def dot(a, b):
    return jnp.dot(a, b, preferred_element_type=F32)


def project_kernel(rhs, bases, mine, other, stack, high, middle, low, sems):
    width = rhs.shape[1] // CHUNKS
    copies = []
    for chunk in range(CHUNKS):
        columns = pl.ds(chunk * width, width)
        copies.append([pltpu.make_async_copy(rhs.at[:, columns], stack.at[: 2 * R, columns], sems.at[0, chunk])])
        for level in range(5):
            rows = pl.ds((2 + level) * R, R)
            copies[chunk].append(
                pltpu.make_async_copy(
                    bases.at[level, :, columns], stack.at[rows, columns], sems.at[level + 1, chunk]
                )
            )
        for copy in copies[chunk]:
            copy.start()

    def add(acc, chunk, value):
        if chunk == 0:
            acc[...] = value
        else:
            acc[...] += value

    for chunk in range(CHUNKS):
        columns = slice(chunk * width, (chunk + 1) * width)
        for copy in copies[chunk]:
            copy.wait()
        add(high, chunk, dot_t(stack[: 6 * R, columns], stack[5 * R :, columns]))
        add(middle, chunk, dot_t(stack[: 4 * R, columns], stack[3 * R : 5 * R, columns]))
        add(low, chunk, dot_t(stack[: 2 * R, columns], stack[2 * R : 3 * R, columns]))

    def tile(ref, row, column):
        return ref[row * R : (row + 1) * R, column * R : (column + 1) * R]

    first = lax.axis_index("c") == 0

    def put(position, zero, one):
        rows = slice(ROWS * position, ROWS * (position + 1))
        zero, one = zero.astype(BF16), one.astype(BF16)
        mine[:, rows, :] = jnp.where(first, zero, one).reshape(HALF, ROWS, R)
        other[:, rows, :] = jnp.where(first, one, zero).reshape(HALF, ROWS, R)

    for level, (ref, column) in enumerate([(low, 0), (middle, 0), (middle, 1), (high, 0), (high, 1)]):
        put(level, tile(ref, 0, column), tile(ref, 1, column))
    put(5, tile(high, 2, 1), tile(high, 3, 1))
    put(6, tile(high, 4, 1), tile(high, 5, 1))
    put(7, tile(high, 2, 0), tile(high, 3, 0))
    put(8, tile(middle, 2, 1), tile(middle, 3, 1))
    put(9, tile(high, 4, 0), tile(middle, 2, 0))


def project(rhs, bases):
    hbm = pl.BlockSpec(memory_space=pltpu.HBM)
    whole = pl.BlockSpec(memory_space=pltpu.VMEM)
    return pl.pallas_call(
        project_kernel,
        in_specs=[hbm, hbm],
        out_specs=[whole, whole],
        out_shape=[jax.ShapeDtypeStruct((HALF, 10 * ROWS, R), BF16)] * 2,
        scratch_shapes=[
            pltpu.VMEM((7 * R, rhs.shape[1]), BF16),
            pltpu.VMEM((6 * R, 2 * R), F32),
            pltpu.VMEM((4 * R, 2 * R), F32),
            pltpu.VMEM((2 * R, R), F32),
            pltpu.SemaphoreType.DMA((6, CHUNKS)),
        ],
        compiler_params=pltpu.CompilerParams(vmem_limit_bytes=PROJECT_VMEM_LIMIT),
    )(rhs, bases)


def local_call(kernel, shapes, *arrays):
    whole = pl.BlockSpec(memory_space=pltpu.VMEM)
    return pl.pallas_call(
        kernel,
        in_specs=[whole] * len(arrays),
        out_specs=[whole] * len(shapes),
        out_shape=[jax.ShapeDtypeStruct(shape, dtype) for shape, dtype in shapes],
        compiler_params=pltpu.CompilerParams(vmem_limit_bytes=VMEM_LIMIT),
    )(*arrays)


def chip_kernel(mine, theirs, out):
    out[...] = (mine[...].astype(F32) + theirs[...].astype(F32)).astype(BF16)


def couple_kernel(parts, coupling, out):
    total = parts[0].astype(F32)
    for source in range(1, HALF):
        total += parts[source].astype(F32)
    total = total.astype(BF16)
    proj, gram = total[: 5 * ROWS], total[5 * ROWS :]
    first = dot(gram[: 2 * ROWS], coupling[4, 0])
    second = dot(gram[2 * ROWS : 3 * ROWS], coupling[3, 0])
    third = dot(gram[3 * ROWS : 4 * ROWS], coupling[2, 0])
    last = gram[4 * ROWS :]
    fourth = jnp.where(lax.axis_index("c") == 0, dot(last, coupling[3, 0]), dot(last, coupling[1, 0]))
    mixed = [first[:ROWS], first[ROWS:], second, third, fourth]
    halves = [m[:, R * half : R * (half + 1)].astype(BF16) for m in mixed for half in (0, 1)]
    whole = jnp.concatenate([proj] + halves, axis=0)
    for copy in range(4):
        out[copy] = whole


def quarter_sum(quarters, start, stop):
    rows = slice(ROWS * start, ROWS * stop)
    return sum((quarters[x, rows].astype(F32) for x in range(1, 4)), quarters[0, rows].astype(F32))


def plane_kernel(quarters, out):
    total = quarter_sum(quarters, 11, 15).astype(BF16)
    for plane in range(4):
        second, first = plane % 2, 2 + plane // 2
        out[plane, :ROWS] = total[ROWS * second : ROWS * (second + 1)]
        out[plane, ROWS:] = total[ROWS * first : ROWS * (first + 1)]


def nodes_kernel(quarters, planes, coupling, out):
    def put(position, value):
        count = value.shape[0] // ROWS
        out[ROWS * position : ROWS * (position + count)] = value.astype(BF16)

    def quarter(x, start, stop):
        return quarters[x, ROWS * start : ROWS * stop].astype(F32)

    for node in range(2):
        put(4 * node, quarter(2 * node, 5, 9) + quarter(2 * node + 1, 5, 9))
    put(8, quarter_sum(quarters, 9, 11))
    summed = planes[0].astype(F32) + planes[1].astype(F32) + planes[2].astype(F32) + planes[3].astype(F32)
    last = quarter_sum(quarters, 13, 15)
    here = lax.axis_index("c") == 0
    put(10, jnp.where(here, last[:ROWS], summed[ROWS:]))
    put(11, last[ROWS:])
    pair = 2 * (lax.axis_index("zl") // 2)
    put(12, planes[pair, :ROWS].astype(F32) + planes[pair + 1, :ROWS].astype(F32))
    node = lax.axis_index("x") // 2
    four = ROWS * 4, ROWS * 5
    left, right = quarters[2 * node, slice(*four)], quarters[2 * node + 1, slice(*four)]
    put(13, apart(left, right, coupling, 4))


def gathered(ref, position):
    rows = slice(ROWS * position, ROWS * (position + 1))
    return jnp.concatenate([ref[2 * y + c, rows] for c in range(2) for y in range(HALF)], axis=0)


def apart(left, right, coupling, level):
    return dot_t(left, coupling[level, 0][:, :R]) + dot_t(right, coupling[level, 0][:, R:])


def levels_kernel(quarters, mixed, coupling, out, keep):
    def proj(x, level):
        return quarters[x, ROWS * level : ROWS * (level + 1)]

    sums = []
    for node in range(2):
        left, right = proj(2 * node, 4), proj(2 * node + 1, 4)
        base = 4 * node
        updates = []
        for part in range(2):
            both = dot_t(left, gathered(mixed, base + 2 * part)) + dot_t(right, gathered(mixed, base + 2 * part + 1))
            updates += [both[:, :R], both[:, R:]]
        sums.append(
            [
                proj(2 * node, l).astype(F32) + proj(2 * node + 1, l).astype(F32) - updates[l]
                for l in range(4)
            ]
        )
    left, right = sums[0][3].astype(BF16), sums[1][3].astype(BF16)
    both = dot_t(left, gathered(mixed, 8)) + dot_t(right, gathered(mixed, 9))
    last = gathered(mixed, 10)
    update = dot_t(left, last[:R]) + dot_t(right, gathered(mixed, 11)[:R])
    two = (sums[0][2] + sums[1][2] - update).astype(BF16)
    lower = dot_t(two, gathered(mixed, 12))
    one = (sums[0][1] + sums[1][1] - both[:, R:] - lower[:, R:]).astype(BF16)
    zero = sums[0][0] + sums[1][0] - both[:, :R] - lower[:, :R] - dot_t(one, last[R:])
    result = jnp.concatenate([zero.astype(BF16), one, two], axis=0)
    for copy in range(8):
        out[copy] = result
    keep[...] = apart(left, right, coupling, 3).astype(BF16)


def corr_kernel(planes, coupling, keep, out):
    def proj(plane, level):
        return planes[plane, ROWS * level : ROWS * (level + 1)]

    def over(level, first, count):
        return sum(
            (proj(first + plane, level).astype(F32) for plane in range(1, count)), proj(first, level).astype(F32)
        ).astype(BF16)

    z = lax.axis_index("zh") * 4 + lax.axis_index("zl")
    pair, quad = 2 * (z // 2), 4 * (z // 4)
    zero = apart(over(0, 0, 4), over(0, 4, 4), coupling, 0).astype(BF16)
    one = apart(over(1, quad, 2), over(1, quad + 2, 2), coupling, 1).astype(BF16)
    two = apart(proj(pair, 2), proj(pair + 1, 2), coupling, 2).astype(BF16)
    result = jnp.concatenate([zero, one, two, keep[...]], axis=0)
    for copy in range(HALF):
        out[copy] = result


def apply_kernel(rhs, bases, mixed, mine, theirs, out, here, sems):
    first = lax.axis_index("c") == 0
    levels = []
    for level in range(4):
        rows = slice(ROWS * level, ROWS * (level + 1))
        low, high = mine[:, rows].reshape(R, R), theirs[:, rows].reshape(R, R)
        levels.append(jnp.concatenate([jnp.where(first, low, high), jnp.where(first, high, low)], axis=0))
    everything = jnp.concatenate(levels + [gathered(mixed, 13)], axis=1)
    width = rhs.shape[1] // OUT_CHUNKS
    copies = []
    for chunk in range(OUT_CHUNKS):
        columns = slice(chunk * width, (chunk + 1) * width)
        update = dot(everything, bases[:, :, columns].reshape(5 * R, width))
        here[:, columns] = (rhs[:, columns].astype(F32) - update).astype(BF16)
        columns = pl.ds(chunk * width, width)
        copies.append(pltpu.make_async_copy(here.at[:, columns], out.at[:, columns], sems.at[chunk]))
        copies[-1].start()
    for copy in copies:
        copy.wait()


def apply_levels(rhs, *arrays):
    whole = pl.BlockSpec(memory_space=pltpu.VMEM)
    return pl.pallas_call(
        apply_kernel,
        in_specs=[whole] * (1 + len(arrays)),
        out_specs=pl.BlockSpec(memory_space=pltpu.HBM),
        out_shape=jax.ShapeDtypeStruct(rhs.shape, BF16),
        scratch_shapes=[pltpu.VMEM(rhs.shape, BF16), pltpu.SemaphoreType.DMA((OUT_CHUNKS,))],
        compiler_params=pltpu.CompilerParams(vmem_limit_bytes=VMEM_LIMIT),
    )(rhs, *arrays)


def on_device(rhs, bases, coupling):
    group = ("y", "c")
    swap = [(0, 1), (1, 0)]
    exchange = functools.partial(lax.all_to_all, split_axis=0, concat_axis=0)

    mine, other = project(rhs, bases)
    theirs = lax.ppermute(other, "c", swap)
    (parts,) = local_call(chip_kernel, [(mine.shape, BF16)], mine, theirs)
    parts = exchange(parts, "y")
    (quarters,) = local_call(couple_kernel, [((4, 15 * ROWS, R), BF16)], parts, coupling)
    quarters = exchange(quarters, "x")
    (planes,) = local_call(plane_kernel, [((4, 2 * ROWS, R), BF16)], quarters)
    planes = exchange(planes, "zl")
    (mixed,) = local_call(nodes_kernel, [((14 * ROWS, R), BF16)], quarters, planes, coupling)
    mixed = lax.all_gather(mixed, group)
    lower, keep = local_call(
        levels_kernel,
        [((8, 3 * ROWS, R), BF16), ((ROWS, R), BF16)],
        quarters,
        mixed,
        coupling,
    )
    lower = exchange(lower, ("zh", "zl"))
    (mine,) = local_call(corr_kernel, [((HALF, 4 * ROWS, R), BF16)], lower, coupling, keep)
    mine = exchange(mine, "y")
    theirs = lax.ppermute(mine, "c", swap)
    return apply_levels(rhs, bases, mixed, mine, theirs)


def solution(mesh):
    names = ("zh", "zl", "x", "y", "c")
    split = Mesh(mesh.devices.reshape(2, 4, 4, 8, 2), names)
    return jax.shard_map(
        on_device,
        mesh=split,
        in_specs=(P(None, names), P(None, None, names), P(None, names, None, None)),
        out_specs=P(None, names),
        check_vma=False,
    )
```

```python
import functools

import jax
import jax.numpy as jnp
from jax import lax
from jax.experimental import pallas as pl
from jax.experimental.pallas import tpu as pltpu
from jax.sharding import Mesh
from jax.sharding import PartitionSpec as P


ROWS = 16
R = 128
CHUNKS = 2
OUT_CHUNKS = 2
HALF = 8
F32 = jnp.float32
BF16 = jnp.bfloat16
VMEM_LIMIT = 40 * 1024 * 1024
PROJECT_VMEM_LIMIT = 53 * 1024 * 1024


def dot_t(a, b):
    return lax.dot_general(a, b, (((1,), (1,)), ((), ())), preferred_element_type=F32)


def dot(a, b):
    return jnp.dot(a, b, preferred_element_type=F32)


def project_kernel(rhs, bases, mine, other, stack, high, middle, low, sems):
    width = rhs.shape[1] // CHUNKS
    copies = []
    for chunk in range(CHUNKS):
        columns = pl.ds(chunk * width, width)
        copies.append([pltpu.make_async_copy(rhs.at[:, columns], stack.at[: 2 * R, columns], sems.at[0, chunk])])
        for level in range(5):
            rows = pl.ds((2 + level) * R, R)
            copies[chunk].append(
                pltpu.make_async_copy(
                    bases.at[level, :, columns], stack.at[rows, columns], sems.at[level + 1, chunk]
                )
            )
        for copy in copies[chunk]:
            copy.start()

    def add(acc, chunk, value):
        if chunk == 0:
            acc[...] = value
        else:
            acc[...] += value

    for chunk in range(CHUNKS):
        columns = slice(chunk * width, (chunk + 1) * width)
        for copy in copies[chunk]:
            copy.wait()
        add(high, chunk, dot_t(stack[: 6 * R, columns], stack[5 * R :, columns]))
        add(middle, chunk, dot_t(stack[: 4 * R, columns], stack[3 * R : 5 * R, columns]))
        add(low, chunk, dot_t(stack[: 2 * R, columns], stack[2 * R : 3 * R, columns]))

    def tile(ref, row, column):
        return ref[row * R : (row + 1) * R, column * R : (column + 1) * R]

    first = lax.axis_index("c") == 0

    def put(position, zero, one):
        rows = slice(ROWS * position, ROWS * (position + 1))
        zero, one = zero.astype(BF16), one.astype(BF16)
        mine[:, rows, :] = jnp.where(first, zero, one).reshape(HALF, ROWS, R)
        other[:, rows, :] = jnp.where(first, one, zero).reshape(HALF, ROWS, R)

    for level, (ref, column) in enumerate([(low, 0), (middle, 0), (middle, 1), (high, 0), (high, 1)]):
        put(level, tile(ref, 0, column), tile(ref, 1, column))
    put(5, tile(high, 2, 1), tile(high, 3, 1))
    put(6, tile(high, 4, 1), tile(high, 5, 1))
    put(7, tile(high, 2, 0), tile(high, 3, 0))
    put(8, tile(middle, 2, 1), tile(middle, 3, 1))
    put(9, tile(high, 4, 0), tile(middle, 2, 0))


def project(rhs, bases):
    hbm = pl.BlockSpec(memory_space=pltpu.HBM)
    whole = pl.BlockSpec(memory_space=pltpu.VMEM)
    return pl.pallas_call(
        project_kernel,
        in_specs=[hbm, hbm],
        out_specs=[whole, whole],
        out_shape=[jax.ShapeDtypeStruct((HALF, 10 * ROWS, R), BF16)] * 2,
        scratch_shapes=[
            pltpu.VMEM((7 * R, rhs.shape[1]), BF16),
            pltpu.VMEM((6 * R, 2 * R), F32),
            pltpu.VMEM((4 * R, 2 * R), F32),
            pltpu.VMEM((2 * R, R), F32),
            pltpu.SemaphoreType.DMA((6, CHUNKS)),
        ],
        compiler_params=pltpu.CompilerParams(vmem_limit_bytes=PROJECT_VMEM_LIMIT),
    )(rhs, bases)


def local_call(kernel, shapes, *arrays):
    whole = pl.BlockSpec(memory_space=pltpu.VMEM)
    return pl.pallas_call(
        kernel,
        in_specs=[whole] * len(arrays),
        out_specs=[whole] * len(shapes),
        out_shape=[jax.ShapeDtypeStruct(shape, dtype) for shape, dtype in shapes],
        compiler_params=pltpu.CompilerParams(vmem_limit_bytes=VMEM_LIMIT),
    )(*arrays)


def chip_kernel(mine, theirs, out):
    out[...] = (mine[...].astype(F32) + theirs[...].astype(F32)).astype(BF16)


def couple_kernel(parts, coupling, out):
    total = parts[0].astype(F32)
    for source in range(1, HALF):
        total += parts[source].astype(F32)
    total = total.astype(BF16)
    proj, gram = total[: 5 * ROWS], total[5 * ROWS :]
    first = dot(gram[: 2 * ROWS], coupling[4, 0])
    second = dot(gram[2 * ROWS : 3 * ROWS], coupling[3, 0])
    third = dot(gram[3 * ROWS : 4 * ROWS], coupling[2, 0])
    last = gram[4 * ROWS :]
    fourth = jnp.where(lax.axis_index("c") == 0, dot(last, coupling[3, 0]), dot(last, coupling[1, 0]))
    mixed = [first[:ROWS], first[ROWS:], second, third, fourth]
    halves = [m[:, R * half : R * (half + 1)].astype(BF16) for m in mixed for half in (0, 1)]
    whole = jnp.concatenate([proj] + halves, axis=0)
    for copy in range(4):
        out[copy] = whole


def quarter_sum(quarters, start, stop):
    rows = slice(ROWS * start, ROWS * stop)
    return sum((quarters[x, rows].astype(F32) for x in range(1, 4)), quarters[0, rows].astype(F32))


def plane_kernel(quarters, out):
    total = quarter_sum(quarters, 11, 15).astype(BF16)
    for plane in range(4):
        second, first = plane % 2, 2 + plane // 2
        out[plane, :ROWS] = total[ROWS * second : ROWS * (second + 1)]
        out[plane, ROWS:] = total[ROWS * first : ROWS * (first + 1)]


def nodes_kernel(quarters, planes, coupling, out):
    def put(position, value):
        count = value.shape[0] // ROWS
        out[ROWS * position : ROWS * (position + count)] = value.astype(BF16)

    def quarter(x, start, stop):
        return quarters[x, ROWS * start : ROWS * stop].astype(F32)

    for node in range(2):
        put(4 * node, quarter(2 * node, 5, 9) + quarter(2 * node + 1, 5, 9))
    put(8, quarter_sum(quarters, 9, 11))
    summed = planes[0].astype(F32) + planes[1].astype(F32) + planes[2].astype(F32) + planes[3].astype(F32)
    last = quarter_sum(quarters, 13, 15)
    here = lax.axis_index("c") == 0
    put(10, jnp.where(here, last[:ROWS], summed[ROWS:]))
    put(11, last[ROWS:])
    pair = 2 * (lax.axis_index("zl") // 2)
    put(12, planes[pair, :ROWS].astype(F32) + planes[pair + 1, :ROWS].astype(F32))
    node = lax.axis_index("x") // 2
    four = ROWS * 4, ROWS * 5
    left, right = quarters[2 * node, slice(*four)], quarters[2 * node + 1, slice(*four)]
    put(13, apart(left, right, coupling, 4))


def gathered(ref, position):
    rows = slice(ROWS * position, ROWS * (position + 1))
    return jnp.concatenate([ref[2 * y + c, rows] for c in range(2) for y in range(HALF)], axis=0)


def apart(left, right, coupling, level):
    return dot_t(left, coupling[level, 0][:, :R]) + dot_t(right, coupling[level, 0][:, R:])


def levels_kernel(quarters, mixed, coupling, out, keep):
    def proj(x, level):
        return quarters[x, ROWS * level : ROWS * (level + 1)]

    sums = []
    for node in range(2):
        left, right = proj(2 * node, 4), proj(2 * node + 1, 4)
        base = 4 * node
        updates = []
        for part in range(2):
            both = dot_t(left, gathered(mixed, base + 2 * part)) + dot_t(right, gathered(mixed, base + 2 * part + 1))
            updates += [both[:, :R], both[:, R:]]
        sums.append(
            [
                proj(2 * node, l).astype(F32) + proj(2 * node + 1, l).astype(F32) - updates[l]
                for l in range(4)
            ]
        )
    left, right = sums[0][3].astype(BF16), sums[1][3].astype(BF16)
    both = dot_t(left, gathered(mixed, 8)) + dot_t(right, gathered(mixed, 9))
    last = gathered(mixed, 10)
    update = dot_t(left, last[:R]) + dot_t(right, gathered(mixed, 11)[:R])
    two = (sums[0][2] + sums[1][2] - update).astype(BF16)
    lower = dot_t(two, gathered(mixed, 12))
    one = (sums[0][1] + sums[1][1] - both[:, R:] - lower[:, R:]).astype(BF16)
    zero = sums[0][0] + sums[1][0] - both[:, :R] - lower[:, :R] - dot_t(one, last[R:])
    result = jnp.concatenate([zero.astype(BF16), one, two], axis=0)
    for copy in range(8):
        out[copy] = result
    keep[...] = apart(left, right, coupling, 3).astype(BF16)


def corr_kernel(planes, coupling, keep, out):
    def proj(plane, level):
        return planes[plane, ROWS * level : ROWS * (level + 1)]

    def over(level, first, count):
        return sum(
            (proj(first + plane, level).astype(F32) for plane in range(1, count)), proj(first, level).astype(F32)
        ).astype(BF16)

    z = lax.axis_index("zh") * 4 + lax.axis_index("zl")
    pair, quad = 2 * (z // 2), 4 * (z // 4)
    zero = apart(over(0, 0, 4), over(0, 4, 4), coupling, 0).astype(BF16)
    one = apart(over(1, quad, 2), over(1, quad + 2, 2), coupling, 1).astype(BF16)
    two = apart(proj(pair, 2), proj(pair + 1, 2), coupling, 2).astype(BF16)
    result = jnp.concatenate([zero, one, two, keep[...]], axis=0)
    for copy in range(2 * HALF):
        out[copy] = result


def apply_kernel(rhs, bases, mixed, corr, out, here, sems):
    levels = [gathered(corr, level) for level in range(4)] + [gathered(mixed, 13)]
    everything = jnp.concatenate(levels, axis=1)
    width = rhs.shape[1] // OUT_CHUNKS
    copies = []
    for chunk in range(OUT_CHUNKS):
        columns = slice(chunk * width, (chunk + 1) * width)
        update = dot(everything, bases[:, :, columns].reshape(5 * R, width))
        here[:, columns] = (rhs[:, columns].astype(F32) - update).astype(BF16)
        columns = pl.ds(chunk * width, width)
        copies.append(pltpu.make_async_copy(here.at[:, columns], out.at[:, columns], sems.at[chunk]))
        copies[-1].start()
    for copy in copies:
        copy.wait()


def apply_levels(rhs, *arrays):
    whole = pl.BlockSpec(memory_space=pltpu.VMEM)
    return pl.pallas_call(
        apply_kernel,
        in_specs=[whole] * (1 + len(arrays)),
        out_specs=pl.BlockSpec(memory_space=pltpu.HBM),
        out_shape=jax.ShapeDtypeStruct(rhs.shape, BF16),
        scratch_shapes=[pltpu.VMEM(rhs.shape, BF16), pltpu.SemaphoreType.DMA((OUT_CHUNKS,))],
        compiler_params=pltpu.CompilerParams(vmem_limit_bytes=VMEM_LIMIT),
    )(rhs, *arrays)


def on_device(rhs, bases, coupling):
    group = ("y", "c")
    swap = [(0, 1), (1, 0)]
    exchange = functools.partial(lax.all_to_all, split_axis=0, concat_axis=0)

    mine, other = project(rhs, bases)
    theirs = lax.ppermute(other, "c", swap)
    (parts,) = local_call(chip_kernel, [(mine.shape, BF16)], mine, theirs)
    parts = exchange(parts, "y")
    (quarters,) = local_call(couple_kernel, [((4, 15 * ROWS, R), BF16)], parts, coupling)
    quarters = exchange(quarters, "x")
    (planes,) = local_call(plane_kernel, [((4, 2 * ROWS, R), BF16)], quarters)
    planes = exchange(planes, "zl")
    (mixed,) = local_call(nodes_kernel, [((14 * ROWS, R), BF16)], quarters, planes, coupling)
    mixed = lax.all_gather(mixed, group)
    lower, keep = local_call(
        levels_kernel,
        [((8, 3 * ROWS, R), BF16), ((ROWS, R), BF16)],
        quarters,
        mixed,
        coupling,
    )
    lower = exchange(lower, ("zh", "zl"))
    (corr,) = local_call(corr_kernel, [((2 * HALF, 4 * ROWS, R), BF16)], lower, coupling, keep)
    return apply_levels(rhs, bases, mixed, exchange(corr, group))


def solution(mesh):
    names = ("zh", "zl", "x", "y", "c")
    split = Mesh(mesh.devices.reshape(2, 4, 4, 8, 2), names)
    return jax.shard_map(
        on_device,
        mesh=split,
        in_specs=(P(None, names), P(None, None, names), P(None, names, None, None)),
        out_specs=P(None, names),
        check_vma=False,
    )
```

```python
import functools

import jax
import jax.numpy as jnp
from jax import lax
from jax.experimental import pallas as pl
from jax.experimental.pallas import tpu as pltpu
from jax.sharding import Mesh
from jax.sharding import PartitionSpec as P


ROWS = 16
R = 128
CHUNKS = 2
OUT_CHUNKS = 2
HALF = 8
F32 = jnp.float32
BF16 = jnp.bfloat16
VMEM_LIMIT = 40 * 1024 * 1024
PROJECT_VMEM_LIMIT = 53 * 1024 * 1024


def dot_t(a, b):
    return lax.dot_general(a, b, (((1,), (1,)), ((), ())), preferred_element_type=F32)


def dot(a, b):
    return jnp.dot(a, b, preferred_element_type=F32)


def project_kernel(rhs, bases, mine, other, stack, high, middle, low, sems):
    width = rhs.shape[1] // CHUNKS
    copies = []
    for chunk in range(CHUNKS):
        columns = pl.ds(chunk * width, width)
        copies.append([pltpu.make_async_copy(rhs.at[:, columns], stack.at[: 2 * R, columns], sems.at[0, chunk])])
        for level in range(5):
            rows = pl.ds((2 + level) * R, R)
            copies[chunk].append(
                pltpu.make_async_copy(
                    bases.at[level, :, columns], stack.at[rows, columns], sems.at[level + 1, chunk]
                )
            )
        for copy in copies[chunk]:
            copy.start()

    def add(acc, chunk, value):
        if chunk == 0:
            acc[...] = value
        else:
            acc[...] += value

    for chunk in range(CHUNKS):
        columns = slice(chunk * width, (chunk + 1) * width)
        for copy in copies[chunk]:
            copy.wait()
        add(high, chunk, dot_t(stack[: 6 * R, columns], stack[5 * R :, columns]))
        add(middle, chunk, dot_t(stack[: 4 * R, columns], stack[3 * R : 5 * R, columns]))
        add(low, chunk, dot_t(stack[: 2 * R, columns], stack[2 * R : 3 * R, columns]))

    def tile(ref, row, column):
        return ref[row * R : (row + 1) * R, column * R : (column + 1) * R]

    first = lax.axis_index("c") == 0

    def put(position, zero, one):
        rows = slice(ROWS * position, ROWS * (position + 1))
        zero, one = zero.astype(BF16), one.astype(BF16)
        mine[:, rows, :] = jnp.where(first, zero, one).reshape(HALF, ROWS, R)
        other[:, rows, :] = jnp.where(first, one, zero).reshape(HALF, ROWS, R)

    for level, (ref, column) in enumerate([(low, 0), (middle, 0), (middle, 1), (high, 0), (high, 1)]):
        put(level, tile(ref, 0, column), tile(ref, 1, column))
    put(5, tile(high, 2, 1), tile(high, 4, 1))
    put(6, tile(high, 3, 1), tile(high, 5, 1))
    put(7, tile(high, 2, 0), tile(middle, 2, 1))
    put(8, tile(high, 3, 0), tile(middle, 3, 1))
    put(9, tile(high, 4, 0), tile(middle, 2, 0))


def project(rhs, bases):
    hbm = pl.BlockSpec(memory_space=pltpu.HBM)
    whole = pl.BlockSpec(memory_space=pltpu.VMEM)
    return pl.pallas_call(
        project_kernel,
        in_specs=[hbm, hbm],
        out_specs=[whole, whole],
        out_shape=[jax.ShapeDtypeStruct((HALF, 10 * ROWS, R), BF16)] * 2,
        scratch_shapes=[
            pltpu.VMEM((7 * R, rhs.shape[1]), BF16),
            pltpu.VMEM((6 * R, 2 * R), F32),
            pltpu.VMEM((4 * R, 2 * R), F32),
            pltpu.VMEM((2 * R, R), F32),
            pltpu.SemaphoreType.DMA((6, CHUNKS)),
        ],
        compiler_params=pltpu.CompilerParams(vmem_limit_bytes=PROJECT_VMEM_LIMIT),
    )(rhs, bases)


def local_call(kernel, shapes, *arrays):
    whole = pl.BlockSpec(memory_space=pltpu.VMEM)
    return pl.pallas_call(
        kernel,
        in_specs=[whole] * len(arrays),
        out_specs=[whole] * len(shapes),
        out_shape=[jax.ShapeDtypeStruct(shape, dtype) for shape, dtype in shapes],
        compiler_params=pltpu.CompilerParams(vmem_limit_bytes=VMEM_LIMIT),
    )(*arrays)


def chip_kernel(mine, theirs, out):
    out[...] = (mine[...].astype(F32) + theirs[...].astype(F32)).astype(BF16)


def couple_kernel(parts, coupling, out):
    total = parts[0].astype(F32)
    for source in range(1, HALF):
        total += parts[source].astype(F32)
    total = total.astype(BF16)
    proj, gram = total[: 5 * ROWS], total[5 * ROWS :]
    first = lax.axis_index("c") == 0
    middle, last = gram[2 * ROWS : 4 * ROWS], gram[4 * ROWS :]
    mixed = [
        dot(gram[: 2 * ROWS], coupling[4, 0]),
        jnp.where(first, dot(middle, coupling[3, 0]), dot(middle, coupling[2, 0])),
        jnp.where(first, dot(last, coupling[3, 0]), dot(last, coupling[1, 0])),
    ]
    mixed = [mixed[0][:ROWS], mixed[0][ROWS:], mixed[1][:ROWS], mixed[1][ROWS:], mixed[2]]
    halves = [m[:, R * half : R * (half + 1)].astype(BF16) for m in mixed for half in (0, 1)]
    whole = jnp.concatenate([proj] + halves, axis=0)
    for copy in range(4):
        out[copy] = whole


def quarter_sum(quarters, start, stop):
    rows = slice(ROWS * start, ROWS * stop)
    return sum((quarters[x, rows].astype(F32) for x in range(1, 4)), quarters[0, rows].astype(F32))


def plane_kernel(quarters, out):
    total = quarter_sum(quarters, 9, 15).astype(BF16)
    for plane in range(4):
        for position, block in enumerate((plane % 2, 2 + plane % 2, 4 + plane // 2)):
            out[plane, ROWS * position : ROWS * (position + 1)] = total[ROWS * block : ROWS * (block + 1)]


def nodes_kernel(quarters, planes, coupling, out):
    def put(position, value):
        count = value.shape[0] // ROWS
        out[ROWS * position : ROWS * (position + count)] = value.astype(BF16)

    def quarter(x, start, stop):
        return quarters[x, ROWS * start : ROWS * stop].astype(F32)

    def over(planes_of, rows):
        return sum((planes[plane, rows].astype(F32) for plane in planes_of[1:]), planes[planes_of[0], rows].astype(F32))

    for node in range(2):
        put(4 * node, quarter(2 * node, 5, 9) + quarter(2 * node + 1, 5, 9))
    pair = 2 * (lax.axis_index("zl") // 2)
    second = over([pair, pair + 1], slice(0, 2 * ROWS))
    first = over([0, 1, 2, 3], slice(2 * ROWS, 3 * ROWS))
    unused = jnp.zeros((3 * ROWS, R), F32)
    here = lax.axis_index("c") == 0
    put(8, jnp.where(here, quarter_sum(quarters, 9, 15), jnp.concatenate([second, first, unused], axis=0)))
    node = lax.axis_index("x") // 2
    four = slice(4 * ROWS, 5 * ROWS)
    put(14, apart(quarters[2 * node, four], quarters[2 * node + 1, four], coupling, 4))


def of_core(ref, core, *positions):
    return jnp.concatenate(
        [ref[2 * y + core, ROWS * p : ROWS * (p + 1)] for p in positions for y in range(HALF)], axis=0
    )


def gathered(ref, position):
    rows = slice(ROWS * position, ROWS * (position + 1))
    return jnp.concatenate([ref[2 * y + c, rows] for c in range(2) for y in range(HALF)], axis=0)


def apart(left, right, coupling, level):
    return dot_t(left, coupling[level, 0][:, :R]) + dot_t(right, coupling[level, 0][:, R:])


def levels_kernel(quarters, mixed, coupling, out, keep):
    def proj(x, level):
        return quarters[x, ROWS * level : ROWS * (level + 1)]

    sums = []
    for node in range(2):
        left, right = proj(2 * node, 4), proj(2 * node + 1, 4)
        base = 4 * node
        updates = []
        for core in range(2):
            both = dot_t(left, of_core(mixed, core, base, base + 2))
            both += dot_t(right, of_core(mixed, core, base + 1, base + 3))
            updates += [both[:, :R], both[:, R:]]
        sums.append(
            [
                proj(2 * node, l).astype(F32) + proj(2 * node + 1, l).astype(F32) - updates[l]
                for l in range(4)
            ]
        )
    left, right = sums[0][3].astype(BF16), sums[1][3].astype(BF16)
    both = dot_t(left, of_core(mixed, 0, 8, 10)) + dot_t(right, of_core(mixed, 0, 9, 11))
    update = dot_t(left, of_core(mixed, 0, 12)) + dot_t(right, of_core(mixed, 0, 13))
    two = (sums[0][2] + sums[1][2] - update).astype(BF16)
    lower = dot_t(two, of_core(mixed, 1, 8, 9))
    one = (sums[0][1] + sums[1][1] - both[:, R:] - lower[:, R:]).astype(BF16)
    zero = sums[0][0] + sums[1][0] - both[:, :R] - lower[:, :R] - dot_t(one, of_core(mixed, 1, 10))
    result = jnp.concatenate([zero.astype(BF16), one, two], axis=0)
    for copy in range(8):
        out[copy] = result
    keep[...] = apart(left, right, coupling, 3).astype(BF16)


def corr_kernel(planes, coupling, keep, out):
    def proj(plane, level):
        return planes[plane, ROWS * level : ROWS * (level + 1)]

    def over(level, first, count):
        return sum(
            (proj(first + plane, level).astype(F32) for plane in range(1, count)), proj(first, level).astype(F32)
        ).astype(BF16)

    z = lax.axis_index("zh") * 4 + lax.axis_index("zl")
    pair, quad = 2 * (z // 2), 4 * (z // 4)
    zero = apart(over(0, 0, 4), over(0, 4, 4), coupling, 0).astype(BF16)
    one = apart(over(1, quad, 2), over(1, quad + 2, 2), coupling, 1).astype(BF16)
    two = apart(proj(pair, 2), proj(pair + 1, 2), coupling, 2).astype(BF16)
    result = jnp.concatenate([zero, one, two, keep[...]], axis=0)
    for copy in range(2 * HALF):
        out[copy] = result


def apply_kernel(rhs, bases, mixed, corr, out, here, sems):
    levels = [gathered(corr, level) for level in range(4)] + [gathered(mixed, 14)]
    everything = jnp.concatenate(levels, axis=1)
    width = rhs.shape[1] // OUT_CHUNKS
    copies = []
    for chunk in range(OUT_CHUNKS):
        columns = slice(chunk * width, (chunk + 1) * width)
        update = dot(everything, bases[:, :, columns].reshape(5 * R, width))
        here[:, columns] = (rhs[:, columns].astype(F32) - update).astype(BF16)
        columns = pl.ds(chunk * width, width)
        copies.append(pltpu.make_async_copy(here.at[:, columns], out.at[:, columns], sems.at[chunk]))
        copies[-1].start()
    for copy in copies:
        copy.wait()


def apply_levels(rhs, *arrays):
    whole = pl.BlockSpec(memory_space=pltpu.VMEM)
    return pl.pallas_call(
        apply_kernel,
        in_specs=[whole] * (1 + len(arrays)),
        out_specs=pl.BlockSpec(memory_space=pltpu.HBM),
        out_shape=jax.ShapeDtypeStruct(rhs.shape, BF16),
        scratch_shapes=[pltpu.VMEM(rhs.shape, BF16), pltpu.SemaphoreType.DMA((OUT_CHUNKS,))],
        compiler_params=pltpu.CompilerParams(vmem_limit_bytes=VMEM_LIMIT),
    )(rhs, *arrays)


def on_device(rhs, bases, coupling):
    group = ("y", "c")
    swap = [(0, 1), (1, 0)]
    exchange = functools.partial(lax.all_to_all, split_axis=0, concat_axis=0)

    mine, other = project(rhs, bases)
    theirs = lax.ppermute(other, "c", swap)
    (parts,) = local_call(chip_kernel, [(mine.shape, BF16)], mine, theirs)
    parts = exchange(parts, "y")
    (quarters,) = local_call(couple_kernel, [((4, 15 * ROWS, R), BF16)], parts, coupling)
    quarters = exchange(quarters, "x")
    (planes,) = local_call(plane_kernel, [((4, 3 * ROWS, R), BF16)], quarters)
    planes = lax.cond(
        lax.axis_index("c") == 1, lambda pieces: exchange(pieces, "zl"), lambda pieces: pieces, planes
    )
    (mixed,) = local_call(nodes_kernel, [((15 * ROWS, R), BF16)], quarters, planes, coupling)
    mixed = lax.all_gather(mixed, group)
    lower, keep = local_call(
        levels_kernel,
        [((8, 3 * ROWS, R), BF16), ((ROWS, R), BF16)],
        quarters,
        mixed,
        coupling,
    )
    lower = exchange(lower, ("zh", "zl"))
    (corr,) = local_call(corr_kernel, [((2 * HALF, 4 * ROWS, R), BF16)], lower, coupling, keep)
    return apply_levels(rhs, bases, mixed, exchange(corr, group))


def solution(mesh):
    names = ("zh", "zl", "x", "y", "c")
    split = Mesh(mesh.devices.reshape(2, 4, 4, 8, 2), names)
    return jax.shard_map(
        on_device,
        mesh=split,
        in_specs=(P(None, names), P(None, None, names), P(None, names, None, None)),
        out_specs=P(None, names),
        check_vma=False,
    )
```

```python
import functools

import functools

import jax
import jax.numpy as jnp
from jax import lax
from jax.experimental import pallas as pl
from jax.experimental.pallas import tpu as pltpu
from jax.sharding import Mesh
from jax.sharding import PartitionSpec as P


ROWS = 16
R = 128
CHUNKS = 2
OUT_CHUNKS = 2
HALF = 8
F32 = jnp.float32
BF16 = jnp.bfloat16
VMEM_LIMIT = 40 * 1024 * 1024
PROJECT_VMEM_LIMIT = 53 * 1024 * 1024


def dot_t(a, b):
    return lax.dot_general(a, b, (((1,), (1,)), ((), ())), preferred_element_type=F32)


def dot(a, b):
    return jnp.dot(a, b, preferred_element_type=F32)


def project_kernel(rhs, bases, mine, other, stack, high, middle, low, sems):
    width = rhs.shape[1] // CHUNKS
    copies = []
    for chunk in range(CHUNKS):
        columns = pl.ds(chunk * width, width)
        copies.append([pltpu.make_async_copy(rhs.at[:, columns], stack.at[: 2 * R, columns], sems.at[0, chunk])])
        for level in range(5):
            rows = pl.ds((2 + level) * R, R)
            copies[chunk].append(
                pltpu.make_async_copy(
                    bases.at[level, :, columns], stack.at[rows, columns], sems.at[level + 1, chunk]
                )
            )
        for copy in copies[chunk]:
            copy.start()

    def add(acc, chunk, value):
        if chunk == 0:
            acc[...] = value
        else:
            acc[...] += value

    for chunk in range(CHUNKS):
        columns = slice(chunk * width, (chunk + 1) * width)
        for copy in copies[chunk]:
            copy.wait()
        add(high, chunk, dot_t(stack[: 6 * R, columns], stack[5 * R :, columns]))
        add(middle, chunk, dot_t(stack[: 4 * R, columns], stack[3 * R : 5 * R, columns]))
        add(low, chunk, dot_t(stack[: 2 * R, columns], stack[2 * R : 3 * R, columns]))

    def tile(ref, row, column):
        return ref[row * R : (row + 1) * R, column * R : (column + 1) * R]

    first = lax.axis_index("c") == 0

    def put(position, zero, one):
        rows = slice(ROWS * position, ROWS * (position + 1))
        zero, one = zero.astype(BF16), one.astype(BF16)
        mine[:, rows, :] = jnp.where(first, zero, one).reshape(HALF, ROWS, R)
        other[:, rows, :] = jnp.where(first, one, zero).reshape(HALF, ROWS, R)

    for level, (ref, column) in enumerate([(low, 0), (middle, 0), (middle, 1), (high, 0), (high, 1)]):
        put(level, tile(ref, 0, column), tile(ref, 1, column))
    put(5, tile(high, 2, 1), tile(high, 4, 1))
    put(6, tile(high, 3, 1), tile(high, 5, 1))
    put(7, tile(high, 2, 0), tile(middle, 2, 1))
    put(8, tile(high, 3, 0), tile(middle, 3, 1))
    put(9, tile(high, 4, 0), tile(middle, 2, 0))


def project(rhs, bases):
    hbm = pl.BlockSpec(memory_space=pltpu.HBM)
    whole = pl.BlockSpec(memory_space=pltpu.VMEM)
    return pl.pallas_call(
        project_kernel,
        in_specs=[hbm, hbm],
        out_specs=[whole, whole],
        out_shape=[jax.ShapeDtypeStruct((HALF, 10 * ROWS, R), BF16)] * 2,
        scratch_shapes=[
            pltpu.VMEM((7 * R, rhs.shape[1]), BF16),
            pltpu.VMEM((6 * R, 2 * R), F32),
            pltpu.VMEM((4 * R, 2 * R), F32),
            pltpu.VMEM((2 * R, R), F32),
            pltpu.SemaphoreType.DMA((6, CHUNKS)),
        ],
        compiler_params=pltpu.CompilerParams(vmem_limit_bytes=PROJECT_VMEM_LIMIT),
    )(rhs, bases)


def local_call(kernel, shapes, *arrays):
    whole = pl.BlockSpec(memory_space=pltpu.VMEM)
    return pl.pallas_call(
        kernel,
        in_specs=[whole] * len(arrays),
        out_specs=[whole] * len(shapes),
        out_shape=[jax.ShapeDtypeStruct(shape, dtype) for shape, dtype in shapes],
        compiler_params=pltpu.CompilerParams(vmem_limit_bytes=VMEM_LIMIT),
    )(*arrays)


def chip_kernel(mine, theirs, out):
    out[...] = (mine[...].astype(F32) + theirs[...].astype(F32)).astype(BF16)


def couple_kernel(core, parts, coupling, out):
    total = parts[0].astype(F32)
    for source in range(1, HALF):
        total += parts[source].astype(F32)
    total = total.astype(BF16)
    proj, gram = total[: 5 * ROWS], total[5 * ROWS :]
    levels = (4, 4, 2, 2, 1) if core else (4, 4, 3, 3, 3)
    mixed = [dot(gram[ROWS * p : ROWS * (p + 1)], coupling[level, 0]) for p, level in enumerate(levels)]
    halves = [m[:, R * half : R * (half + 1)].astype(BF16) for m in mixed for half in (0, 1)]
    whole = jnp.concatenate([proj] + halves, axis=0)
    for copy in range(4):
        out[copy] = whole


def quarter_sum(quarters, start, stop):
    rows = slice(ROWS * start, ROWS * stop)
    return sum((quarters[x, rows].astype(F32) for x in range(1, 4)), quarters[0, rows].astype(F32))


def plane_kernel(quarters, out):
    total = quarter_sum(quarters, 9, 15).astype(BF16)
    for plane in range(4):
        for position, block in enumerate((plane % 2, 2 + plane % 2, 4 + plane // 2)):
            out[plane, ROWS * position : ROWS * (position + 1)] = total[ROWS * block : ROWS * (block + 1)]


def nodes_kernel(quarters, coupling, *planes_and_out):
    *planes, proj, out = planes_and_out
    proj[...] = quarters[:, : 5 * ROWS]

    def put(position, value):
        count = value.shape[0] // ROWS
        out[ROWS * position : ROWS * (position + count)] = value.astype(BF16)

    def quarter(x, start, stop):
        return quarters[x, ROWS * start : ROWS * stop].astype(F32)

    for node in range(2):
        put(4 * node, quarter(2 * node, 5, 9) + quarter(2 * node + 1, 5, 9))
    if planes:
        (planes,) = planes
        pair = 2 * (lax.axis_index("zl") // 2)
        second, first = slice(0, 2 * ROWS), slice(2 * ROWS, 3 * ROWS)
        put(8, planes[pair, second].astype(F32) + planes[pair + 1, second].astype(F32))
        put(10, sum((planes[plane, first].astype(F32) for plane in range(1, 4)), planes[0, first].astype(F32)))
        put(11, jnp.zeros((3 * ROWS, R), F32))
    else:
        put(8, quarter_sum(quarters, 9, 15))
    node = lax.axis_index("x") // 2
    four = slice(4 * ROWS, 5 * ROWS)
    put(14, apart(quarters[2 * node, four], quarters[2 * node + 1, four], coupling, 4))


def of_core(ref, core, *positions):
    return jnp.concatenate(
        [ref[2 * y + core, ROWS * p : ROWS * (p + 1)] for p in positions for y in range(HALF)], axis=0
    )


def gathered(ref, position):
    rows = slice(ROWS * position, ROWS * (position + 1))
    return jnp.concatenate([ref[2 * y + c, rows] for c in range(2) for y in range(HALF)], axis=0)


def apart(left, right, coupling, level):
    return dot_t(left, coupling[level, 0][:, :R]) + dot_t(right, coupling[level, 0][:, R:])


def levels_kernel(quarters, mixed, coupling, out, keep):
    def proj(x, level):
        return quarters[x, ROWS * level : ROWS * (level + 1)]

    sums = []
    for node in range(2):
        left, right = proj(2 * node, 4), proj(2 * node + 1, 4)
        base = 4 * node
        updates = []
        for core in range(2):
            both = dot_t(left, of_core(mixed, core, base, base + 2))
            both += dot_t(right, of_core(mixed, core, base + 1, base + 3))
            updates += [both[:, :R], both[:, R:]]
        sums.append(
            [
                proj(2 * node, l).astype(F32) + proj(2 * node + 1, l).astype(F32) - updates[l]
                for l in range(4)
            ]
        )
    left, right = sums[0][3].astype(BF16), sums[1][3].astype(BF16)
    both = dot_t(left, of_core(mixed, 0, 8, 10)) + dot_t(right, of_core(mixed, 0, 9, 11))
    update = dot_t(left, of_core(mixed, 0, 12)) + dot_t(right, of_core(mixed, 0, 13))
    two = (sums[0][2] + sums[1][2] - update).astype(BF16)
    lower = dot_t(two, of_core(mixed, 1, 8, 9))
    one = (sums[0][1] + sums[1][1] - both[:, R:] - lower[:, R:]).astype(BF16)
    zero = sums[0][0] + sums[1][0] - both[:, :R] - lower[:, :R] - dot_t(one, of_core(mixed, 1, 10))
    result = jnp.concatenate([zero.astype(BF16), one, two], axis=0)
    for copy in range(8):
        out[copy] = result
    keep[...] = apart(left, right, coupling, 3).astype(BF16)


def corr_kernel(planes, coupling, keep, out):
    def proj(plane, level):
        return planes[plane, ROWS * level : ROWS * (level + 1)]

    def over(level, first, count):
        return sum(
            (proj(first + plane, level).astype(F32) for plane in range(1, count)), proj(first, level).astype(F32)
        ).astype(BF16)

    z = lax.axis_index("zh") * 4 + lax.axis_index("zl")
    pair, quad = 2 * (z // 2), 4 * (z // 4)
    zero = apart(over(0, 0, 4), over(0, 4, 4), coupling, 0).astype(BF16)
    one = apart(over(1, quad, 2), over(1, quad + 2, 2), coupling, 1).astype(BF16)
    two = apart(proj(pair, 2), proj(pair + 1, 2), coupling, 2).astype(BF16)
    result = jnp.concatenate([zero, one, two, keep[...]], axis=0)
    for copy in range(2 * HALF):
        out[copy] = result


def apply_kernel(rhs, bases, mixed, corr, out, here, sems):
    levels = [gathered(corr, level) for level in range(4)] + [gathered(mixed, 14)]
    everything = jnp.concatenate(levels, axis=1)
    width = rhs.shape[1] // OUT_CHUNKS
    copies = []
    for chunk in range(OUT_CHUNKS):
        columns = slice(chunk * width, (chunk + 1) * width)
        update = dot(everything, bases[:, :, columns].reshape(5 * R, width))
        here[:, columns] = (rhs[:, columns].astype(F32) - update).astype(BF16)
        columns = pl.ds(chunk * width, width)
        copies.append(pltpu.make_async_copy(here.at[:, columns], out.at[:, columns], sems.at[chunk]))
        copies[-1].start()
    for copy in copies:
        copy.wait()


def apply_levels(rhs, *arrays):
    whole = pl.BlockSpec(memory_space=pltpu.VMEM)
    return pl.pallas_call(
        apply_kernel,
        in_specs=[whole] * (1 + len(arrays)),
        out_specs=pl.BlockSpec(memory_space=pltpu.HBM),
        out_shape=jax.ShapeDtypeStruct(rhs.shape, BF16),
        scratch_shapes=[pltpu.VMEM(rhs.shape, BF16), pltpu.SemaphoreType.DMA((OUT_CHUNKS,))],
        compiler_params=pltpu.CompilerParams(vmem_limit_bytes=VMEM_LIMIT),
    )(rhs, *arrays)


def on_device(rhs, bases, coupling):
    group = ("y", "c")
    swap = [(0, 1), (1, 0)]
    exchange = functools.partial(lax.all_to_all, split_axis=0, concat_axis=0)

    mine, other = project(rhs, bases)
    theirs = lax.ppermute(other, "c", swap)
    (parts,) = local_call(chip_kernel, [(mine.shape, BF16)], mine, theirs)

    def reduce_and_mix(core, parts, coupling):
        parts = exchange(parts, "y")
        couple = functools.partial(couple_kernel, core)
        (quarters,) = local_call(couple, [((4, 15 * ROWS, R), BF16)], parts, coupling)
        quarters = exchange(quarters, "x")
        planes = []
        if core:
            planes = local_call(plane_kernel, [((4, 3 * ROWS, R), BF16)], quarters)
            planes = [exchange(planes[0], "zl")]
        shapes = [((4, 5 * ROWS, R), BF16), ((15 * ROWS, R), BF16)]
        return local_call(nodes_kernel, shapes, quarters, coupling, *planes)

    proj, mixed = lax.cond(
        lax.axis_index("c") == 1,
        functools.partial(reduce_and_mix, 1),
        functools.partial(reduce_and_mix, 0),
        parts,
        coupling,
    )
    mixed = lax.all_gather(mixed, group)
    lower, keep = local_call(
        levels_kernel,
        [((8, 3 * ROWS, R), BF16), ((ROWS, R), BF16)],
        proj,
        mixed,
        coupling,
    )
    lower = exchange(lower, ("zh", "zl"))
    (corr,) = local_call(corr_kernel, [((2 * HALF, 4 * ROWS, R), BF16)], lower, coupling, keep)
    return apply_levels(rhs, bases, mixed, exchange(corr, group))


def solution(mesh):
    names = ("zh", "zl", "x", "y", "c")
    split = Mesh(mesh.devices.reshape(2, 4, 4, 8, 2), names)
    return jax.shard_map(
        on_device,
        mesh=split,
        in_specs=(P(None, names), P(None, None, names), P(None, names, None, None)),
        out_specs=P(None, names),
        check_vma=False,
    )
```

```python
import functools

import functools

import jax
import jax.numpy as jnp
from jax import lax
from jax.experimental import pallas as pl
from jax.experimental.pallas import tpu as pltpu
from jax.sharding import Mesh
from jax.sharding import PartitionSpec as P


ROWS = 16
R = 128
CHUNKS = 2
OUT_CHUNKS = 2
HALF = 8
F32 = jnp.float32
BF16 = jnp.bfloat16
VMEM_LIMIT = 40 * 1024 * 1024
PROJECT_VMEM_LIMIT = 53 * 1024 * 1024


def dot_t(a, b):
    return lax.dot_general(a, b, (((1,), (1,)), ((), ())), preferred_element_type=F32)


def dot(a, b):
    return jnp.dot(a, b, preferred_element_type=F32)


def load(rhs, rhs_rows, bases, stack, sems):
    width = rhs.shape[1] // CHUNKS
    copies = []
    for chunk in range(CHUNKS):
        columns = pl.ds(chunk * width, width)
        count = rhs_rows.stop - rhs_rows.start
        source = rhs.at[pl.ds(rhs_rows.start, count), columns]
        copies.append([pltpu.make_async_copy(source, stack.at[pl.ds(0, count), columns], sems.at[0, chunk])])
        for level in range(5):
            rows = pl.ds(count + level * R, R)
            copies[chunk].append(
                pltpu.make_async_copy(
                    bases.at[level, :, columns], stack.at[rows, columns], sems.at[level + 1, chunk]
                )
            )
        for copy in copies[chunk]:
            copy.start()
    return copies


def multiply(copies, stack, products):
    width = stack.shape[1] // CHUNKS
    for chunk in range(CHUNKS):
        columns = slice(chunk * width, (chunk + 1) * width)
        for copy in copies[chunk]:
            copy.wait()
        for acc, lefts, rights in products:
            value = dot_t(
                stack[lefts.start * R : lefts.stop * R, columns], stack[rights.start * R : rights.stop * R, columns]
            )
            if chunk == 0:
                acc[: value.shape[0]] = value
            else:
                acc[: value.shape[0]] += value


def tile(ref, row, column):
    return ref[row * R : (row + 1) * R, column * R : (column + 1) * R]


def rows_of(position):
    return slice(ROWS * position, ROWS * (position + 1))


def half_products(half, rhs, bases, stack, high, middle, low, sems, put):
    copies = load(rhs, slice(R * half, R * (half + 1)), bases, stack, sems)
    multiply(
        copies,
        stack,
        [(high, slice(0, 5), slice(4, 6)), (middle, slice(0, 3), slice(2, 4)), (low, slice(0, 1), slice(1, 2))],
    )
    places = [(low, 0, 0), (middle, 0, 0), (middle, 0, 1), (high, 0, 0), (high, 0, 1)]
    if half == 0:
        places += [(high, 1, 1), (high, 2, 1), (high, 1, 0), (high, 2, 0), (high, 3, 0)]
    else:
        places += [(high, 3, 1), (high, 4, 1), (middle, 1, 1), (middle, 2, 1), (middle, 1, 0)]
    for position, place in enumerate(places):
        put(position, tile(*place))


def project_kernel(rhs, bases, mine, other, stack, high, middle, low, sems):
    core = lax.axis_index("c")

    @pl.when(core == 0)
    def _():
        def put(position, value):
            other[:, rows_of(position), :] = value.astype(BF16).reshape(HALF, ROWS, R)

        half_products(1, rhs, bases, stack, high, middle, low, sems, put)
        mine[...] = jnp.zeros_like(mine)

    @pl.when(core == 1)
    def _():
        def put(position, zero, one):
            other[:, rows_of(position), :] = zero.astype(BF16).reshape(HALF, ROWS, R)
            mine[:, rows_of(position), :] = one.astype(BF16).reshape(HALF, ROWS, R)

        copies = load(rhs, slice(0, 2 * R), bases, stack, sems)
        multiply(
            copies,
            stack,
            [(high, slice(0, 6), slice(5, 7)), (middle, slice(0, 4), slice(3, 5)), (low, slice(0, 2), slice(2, 3))],
        )
        for level, (ref, column) in enumerate([(low, 0), (middle, 0), (middle, 1), (high, 0), (high, 1)]):
            put(level, tile(ref, 0, column), tile(ref, 1, column))
        put(5, tile(high, 2, 1), tile(high, 4, 1))
        put(6, tile(high, 3, 1), tile(high, 5, 1))
        put(7, tile(high, 2, 0), tile(middle, 2, 1))
        put(8, tile(high, 3, 0), tile(middle, 3, 1))
        put(9, tile(high, 4, 0), tile(middle, 2, 0))


def own_kernel(rhs, bases, theirs, out, stack, high, middle, low, sems):
    def put(position, value):
        rows = rows_of(position)
        out[:, rows, :] = (value.reshape(HALF, ROWS, R) + theirs[:, rows, :].astype(F32)).astype(BF16)

    half_products(0, rhs, bases, stack, high, middle, low, sems, put)


def project(kernel, outputs, rhs, bases, *theirs):
    hbm = pl.BlockSpec(memory_space=pltpu.HBM)
    whole = pl.BlockSpec(memory_space=pltpu.VMEM)
    return pl.pallas_call(
        kernel,
        in_specs=[hbm, hbm] + [whole] * len(theirs),
        out_specs=[whole] * outputs,
        out_shape=[jax.ShapeDtypeStruct((HALF, 10 * ROWS, R), BF16)] * outputs,
        scratch_shapes=[
            pltpu.VMEM((7 * R, rhs.shape[1]), BF16),
            pltpu.VMEM((6 * R, 2 * R), F32),
            pltpu.VMEM((4 * R, 2 * R), F32),
            pltpu.VMEM((2 * R, R), F32),
            pltpu.SemaphoreType.DMA((6, CHUNKS)),
        ],
        compiler_params=pltpu.CompilerParams(vmem_limit_bytes=PROJECT_VMEM_LIMIT),
    )(rhs, bases, *theirs)


def local_call(kernel, shapes, *arrays):
    whole = pl.BlockSpec(memory_space=pltpu.VMEM)
    return pl.pallas_call(
        kernel,
        in_specs=[whole] * len(arrays),
        out_specs=[whole] * len(shapes),
        out_shape=[jax.ShapeDtypeStruct(shape, dtype) for shape, dtype in shapes],
        compiler_params=pltpu.CompilerParams(vmem_limit_bytes=VMEM_LIMIT),
    )(*arrays)


def chip_kernel(mine, theirs, out):
    out[...] = (mine[...].astype(F32) + theirs[...].astype(F32)).astype(BF16)


def couple_kernel(core, parts, coupling, out):
    total = parts[0].astype(F32)
    for source in range(1, HALF):
        total += parts[source].astype(F32)
    total = total.astype(BF16)
    proj, gram = total[: 5 * ROWS], total[5 * ROWS :]
    levels = (4, 4, 2, 2, 1) if core else (4, 4, 3, 3, 3)
    mixed = [dot(gram[ROWS * p : ROWS * (p + 1)], coupling[level, 0]) for p, level in enumerate(levels)]
    halves = [m[:, R * half : R * (half + 1)].astype(BF16) for m in mixed for half in (0, 1)]
    whole = jnp.concatenate([proj] + halves, axis=0)
    for copy in range(4):
        out[copy] = whole


def quarter_sum(quarters, start, stop):
    rows = slice(ROWS * start, ROWS * stop)
    return sum((quarters[x, rows].astype(F32) for x in range(1, 4)), quarters[0, rows].astype(F32))


def plane_kernel(quarters, out):
    total = quarter_sum(quarters, 9, 15).astype(BF16)
    for plane in range(4):
        for position, block in enumerate((plane % 2, 2 + plane % 2, 4 + plane // 2)):
            out[plane, ROWS * position : ROWS * (position + 1)] = total[ROWS * block : ROWS * (block + 1)]


def nodes_kernel(quarters, coupling, *planes_and_out):
    *planes, proj, out = planes_and_out
    proj[...] = quarters[:, : 5 * ROWS]

    def put(position, value):
        count = value.shape[0] // ROWS
        out[ROWS * position : ROWS * (position + count)] = value.astype(BF16)

    def quarter(x, start, stop):
        return quarters[x, ROWS * start : ROWS * stop].astype(F32)

    for node in range(2):
        put(4 * node, quarter(2 * node, 5, 9) + quarter(2 * node + 1, 5, 9))
    if planes:
        (planes,) = planes
        pair = 2 * (lax.axis_index("zl") // 2)
        second, first = slice(0, 2 * ROWS), slice(2 * ROWS, 3 * ROWS)
        put(8, planes[pair, second].astype(F32) + planes[pair + 1, second].astype(F32))
        put(10, sum((planes[plane, first].astype(F32) for plane in range(1, 4)), planes[0, first].astype(F32)))
        put(11, jnp.zeros((3 * ROWS, R), F32))
    else:
        put(8, quarter_sum(quarters, 9, 15))
    node = lax.axis_index("x") // 2
    four = slice(4 * ROWS, 5 * ROWS)
    put(14, apart(quarters[2 * node, four], quarters[2 * node + 1, four], coupling, 4))


def of_core(ref, core, *positions):
    return jnp.concatenate(
        [ref[2 * y + core, ROWS * p : ROWS * (p + 1)] for p in positions for y in range(HALF)], axis=0
    )


def gathered(ref, position):
    rows = slice(ROWS * position, ROWS * (position + 1))
    return jnp.concatenate([ref[2 * y + c, rows] for c in range(2) for y in range(HALF)], axis=0)


def apart(left, right, coupling, level):
    return dot_t(left, coupling[level, 0][:, :R]) + dot_t(right, coupling[level, 0][:, R:])


def levels_kernel(quarters, mixed, coupling, out, keep):
    def proj(x, level):
        return quarters[x, ROWS * level : ROWS * (level + 1)]

    sums = []
    for node in range(2):
        left, right = proj(2 * node, 4), proj(2 * node + 1, 4)
        base = 4 * node
        updates = []
        for core in range(2):
            both = dot_t(left, of_core(mixed, core, base, base + 2))
            both += dot_t(right, of_core(mixed, core, base + 1, base + 3))
            updates += [both[:, :R], both[:, R:]]
        sums.append(
            [
                proj(2 * node, l).astype(F32) + proj(2 * node + 1, l).astype(F32) - updates[l]
                for l in range(4)
            ]
        )
    left, right = sums[0][3].astype(BF16), sums[1][3].astype(BF16)
    both = dot_t(left, of_core(mixed, 0, 8, 10)) + dot_t(right, of_core(mixed, 0, 9, 11))
    update = dot_t(left, of_core(mixed, 0, 12)) + dot_t(right, of_core(mixed, 0, 13))
    two = (sums[0][2] + sums[1][2] - update).astype(BF16)
    lower = dot_t(two, of_core(mixed, 1, 8, 9))
    one = (sums[0][1] + sums[1][1] - both[:, R:] - lower[:, R:]).astype(BF16)
    zero = sums[0][0] + sums[1][0] - both[:, :R] - lower[:, :R] - dot_t(one, of_core(mixed, 1, 10))
    result = jnp.concatenate([zero.astype(BF16), one, two], axis=0)
    for copy in range(8):
        out[copy] = result
    keep[...] = apart(left, right, coupling, 3).astype(BF16)


def corr_kernel(planes, coupling, keep, out):
    def proj(plane, level):
        return planes[plane, ROWS * level : ROWS * (level + 1)]

    def over(level, first, count):
        return sum(
            (proj(first + plane, level).astype(F32) for plane in range(1, count)), proj(first, level).astype(F32)
        ).astype(BF16)

    z = lax.axis_index("zh") * 4 + lax.axis_index("zl")
    pair, quad = 2 * (z // 2), 4 * (z // 4)
    zero = apart(over(0, 0, 4), over(0, 4, 4), coupling, 0).astype(BF16)
    one = apart(over(1, quad, 2), over(1, quad + 2, 2), coupling, 1).astype(BF16)
    two = apart(proj(pair, 2), proj(pair + 1, 2), coupling, 2).astype(BF16)
    result = jnp.concatenate([zero, one, two, keep[...]], axis=0)
    for copy in range(2 * HALF):
        out[copy] = result


def apply_kernel(rhs, bases, mixed, corr, out, here, sems):
    levels = [gathered(corr, level) for level in range(4)] + [gathered(mixed, 14)]
    everything = jnp.concatenate(levels, axis=1)
    width = rhs.shape[1] // OUT_CHUNKS
    copies = []
    for chunk in range(OUT_CHUNKS):
        columns = slice(chunk * width, (chunk + 1) * width)
        update = dot(everything, bases[:, :, columns].reshape(5 * R, width))
        here[:, columns] = (rhs[:, columns].astype(F32) - update).astype(BF16)
        columns = pl.ds(chunk * width, width)
        copies.append(pltpu.make_async_copy(here.at[:, columns], out.at[:, columns], sems.at[chunk]))
        copies[-1].start()
    for copy in copies:
        copy.wait()


def apply_levels(rhs, *arrays):
    whole = pl.BlockSpec(memory_space=pltpu.VMEM)
    return pl.pallas_call(
        apply_kernel,
        in_specs=[whole] * (1 + len(arrays)),
        out_specs=pl.BlockSpec(memory_space=pltpu.HBM),
        out_shape=jax.ShapeDtypeStruct(rhs.shape, BF16),
        scratch_shapes=[pltpu.VMEM(rhs.shape, BF16), pltpu.SemaphoreType.DMA((OUT_CHUNKS,))],
        compiler_params=pltpu.CompilerParams(vmem_limit_bytes=VMEM_LIMIT),
    )(rhs, *arrays)


def on_device(rhs, bases, coupling):
    group = ("y", "c")
    swap = [(0, 1), (1, 0)]
    exchange = functools.partial(lax.all_to_all, split_axis=0, concat_axis=0)

    mine, other = project(project_kernel, 2, rhs, bases)
    theirs = lax.ppermute(other, "c", swap)
    (parts,) = local_call(chip_kernel, [(mine.shape, BF16)], mine, theirs)

    def reduce_and_mix(core, rhs, bases, parts, coupling):
        if not core:
            (parts,) = project(own_kernel, 1, rhs, bases, parts)
        parts = exchange(parts, "y")
        couple = functools.partial(couple_kernel, core)
        (quarters,) = local_call(couple, [((4, 15 * ROWS, R), BF16)], parts, coupling)
        quarters = exchange(quarters, "x")
        planes = []
        if core:
            planes = local_call(plane_kernel, [((4, 3 * ROWS, R), BF16)], quarters)
            planes = [exchange(planes[0], "zl")]
        shapes = [((4, 5 * ROWS, R), BF16), ((15 * ROWS, R), BF16)]
        return local_call(nodes_kernel, shapes, quarters, coupling, *planes)

    proj, mixed = lax.cond(
        lax.axis_index("c") == 1,
        functools.partial(reduce_and_mix, 1),
        functools.partial(reduce_and_mix, 0),
        rhs,
        bases,
        parts,
        coupling,
    )
    mixed = lax.all_gather(mixed, group)
    lower, keep = local_call(
        levels_kernel,
        [((8, 3 * ROWS, R), BF16), ((ROWS, R), BF16)],
        proj,
        mixed,
        coupling,
    )
    lower = exchange(lower, ("zh", "zl"))
    (corr,) = local_call(corr_kernel, [((2 * HALF, 4 * ROWS, R), BF16)], lower, coupling, keep)
    return apply_levels(rhs, bases, mixed, exchange(corr, group))


def solution(mesh):
    names = ("zh", "zl", "x", "y", "c")
    split = Mesh(mesh.devices.reshape(2, 4, 4, 8, 2), names)
    return jax.shard_map(
        on_device,
        mesh=split,
        in_specs=(P(None, names), P(None, None, names), P(None, names, None, None)),
        out_specs=P(None, names),
        check_vma=False,
    )
```

```python
import functools

import functools

import jax
import jax.numpy as jnp
from jax import lax
from jax.experimental import pallas as pl
from jax.experimental.pallas import tpu as pltpu
from jax.sharding import Mesh
from jax.sharding import PartitionSpec as P


ROWS = 16
R = 128
CHUNKS = (768, 1280)
OUT_CHUNKS = 2
HALF = 8
F32 = jnp.float32
BF16 = jnp.bfloat16
VMEM_LIMIT = 40 * 1024 * 1024
PROJECT_VMEM_LIMIT = 53 * 1024 * 1024


def dot_t(a, b):
    return lax.dot_general(a, b, (((1,), (1,)), ((), ())), preferred_element_type=F32)


def dot(a, b):
    return jnp.dot(a, b, preferred_element_type=F32)


def load(rhs, rhs_rows, bases, stack, sems):
    copies = []
    for chunk, width in enumerate(CHUNKS):
        columns = pl.ds(sum(CHUNKS[:chunk]), width)
        count = rhs_rows.stop - rhs_rows.start
        source = rhs.at[pl.ds(rhs_rows.start, count), columns]
        copies.append([pltpu.make_async_copy(source, stack.at[pl.ds(0, count), columns], sems.at[0, chunk])])
        for level in range(5):
            rows = pl.ds(count + level * R, R)
            copies[chunk].append(
                pltpu.make_async_copy(
                    bases.at[level, :, columns], stack.at[rows, columns], sems.at[level + 1, chunk]
                )
            )
        for copy in copies[chunk]:
            copy.start()
    return copies


def multiply(copies, stack, products):
    for chunk, width in enumerate(CHUNKS):
        columns = slice(sum(CHUNKS[:chunk]), sum(CHUNKS[: chunk + 1]))
        for copy in copies[chunk]:
            copy.wait()
        for acc, lefts, rights in products:
            value = dot_t(
                stack[lefts.start * R : lefts.stop * R, columns], stack[rights.start * R : rights.stop * R, columns]
            )
            if chunk == 0:
                acc[: value.shape[0]] = value
            else:
                acc[: value.shape[0]] += value


def tile(ref, row, column):
    return ref[row * R : (row + 1) * R, column * R : (column + 1) * R]


def rows_of(position):
    return slice(ROWS * position, ROWS * (position + 1))


def half_products(half, rhs, bases, stack, high, middle, low, sems, put):
    copies = load(rhs, slice(R * half, R * (half + 1)), bases, stack, sems)
    multiply(
        copies,
        stack,
        [(high, slice(0, 5), slice(4, 6)), (middle, slice(0, 3), slice(2, 4)), (low, slice(0, 1), slice(1, 2))],
    )
    places = [(low, 0, 0), (middle, 0, 0), (middle, 0, 1), (high, 0, 0), (high, 0, 1)]
    if half == 0:
        places += [(high, 1, 1), (high, 2, 1), (high, 1, 0), (high, 2, 0), (high, 3, 0)]
    else:
        places += [(high, 3, 1), (high, 4, 1), (middle, 1, 1), (middle, 2, 1), (middle, 1, 0)]
    for position, place in enumerate(places):
        put(position, tile(*place))


def project_kernel(rhs, bases, mine, other, stack, high, middle, low, sems):
    core = lax.axis_index("c")

    @pl.when(core == 0)
    def _():
        def put(position, value):
            other[:, rows_of(position), :] = value.astype(BF16).reshape(HALF, ROWS, R)

        half_products(1, rhs, bases, stack, high, middle, low, sems, put)
        mine[...] = jnp.zeros_like(mine)

    @pl.when(core == 1)
    def _():
        def put(position, zero, one):
            other[:, rows_of(position), :] = zero.astype(BF16).reshape(HALF, ROWS, R)
            mine[:, rows_of(position), :] = one.astype(BF16).reshape(HALF, ROWS, R)

        copies = load(rhs, slice(0, 2 * R), bases, stack, sems)
        multiply(
            copies,
            stack,
            [(high, slice(0, 6), slice(5, 7)), (middle, slice(0, 4), slice(3, 5)), (low, slice(0, 2), slice(2, 3))],
        )
        for level, (ref, column) in enumerate([(low, 0), (middle, 0), (middle, 1), (high, 0), (high, 1)]):
            put(level, tile(ref, 0, column), tile(ref, 1, column))
        put(5, tile(high, 2, 1), tile(high, 4, 1))
        put(6, tile(high, 3, 1), tile(high, 5, 1))
        put(7, tile(high, 2, 0), tile(middle, 2, 1))
        put(8, tile(high, 3, 0), tile(middle, 3, 1))
        put(9, tile(high, 4, 0), tile(middle, 2, 0))


def own_kernel(rhs, bases, theirs, out, stack, high, middle, low, sems):
    def put(position, value):
        rows = rows_of(position)
        out[:, rows, :] = (value.reshape(HALF, ROWS, R) + theirs[:, rows, :].astype(F32)).astype(BF16)

    half_products(0, rhs, bases, stack, high, middle, low, sems, put)


def project(kernel, outputs, rhs, bases, *theirs):
    hbm = pl.BlockSpec(memory_space=pltpu.HBM)
    whole = pl.BlockSpec(memory_space=pltpu.VMEM)
    return pl.pallas_call(
        kernel,
        in_specs=[hbm, hbm] + [whole] * len(theirs),
        out_specs=[whole] * outputs,
        out_shape=[jax.ShapeDtypeStruct((HALF, 10 * ROWS, R), BF16)] * outputs,
        scratch_shapes=[
            pltpu.VMEM((7 * R, rhs.shape[1]), BF16),
            pltpu.VMEM((6 * R, 2 * R), F32),
            pltpu.VMEM((4 * R, 2 * R), F32),
            pltpu.VMEM((2 * R, R), F32),
            pltpu.SemaphoreType.DMA((6, len(CHUNKS))),
        ],
        compiler_params=pltpu.CompilerParams(vmem_limit_bytes=PROJECT_VMEM_LIMIT),
    )(rhs, bases, *theirs)


def local_call(kernel, shapes, *arrays):
    whole = pl.BlockSpec(memory_space=pltpu.VMEM)
    return pl.pallas_call(
        kernel,
        in_specs=[whole] * len(arrays),
        out_specs=[whole] * len(shapes),
        out_shape=[jax.ShapeDtypeStruct(shape, dtype) for shape, dtype in shapes],
        compiler_params=pltpu.CompilerParams(vmem_limit_bytes=VMEM_LIMIT),
    )(*arrays)


def chip_kernel(mine, theirs, out):
    out[...] = (mine[...].astype(F32) + theirs[...].astype(F32)).astype(BF16)


def couple_kernel(core, parts, coupling, out):
    total = parts[0].astype(F32)
    for source in range(1, HALF):
        total += parts[source].astype(F32)
    total = total.astype(BF16)
    proj, gram = total[: 5 * ROWS], total[5 * ROWS :]
    levels = (4, 4, 2, 2, 1) if core else (4, 4, 3, 3, 3)
    mixed = [dot(gram[ROWS * p : ROWS * (p + 1)], coupling[level, 0]) for p, level in enumerate(levels)]
    halves = [m[:, R * half : R * (half + 1)].astype(BF16) for m in mixed for half in (0, 1)]
    whole = jnp.concatenate([proj] + halves, axis=0)
    for copy in range(4):
        out[copy] = whole


def quarter_sum(quarters, start, stop):
    rows = slice(ROWS * start, ROWS * stop)
    return sum((quarters[x, rows].astype(F32) for x in range(1, 4)), quarters[0, rows].astype(F32))


def plane_kernel(quarters, out):
    total = quarter_sum(quarters, 9, 15).astype(BF16)
    for plane in range(4):
        for position, block in enumerate((plane % 2, 2 + plane % 2, 4 + plane // 2)):
            out[plane, ROWS * position : ROWS * (position + 1)] = total[ROWS * block : ROWS * (block + 1)]


def nodes_kernel(quarters, coupling, *planes_and_out):
    *planes, proj, out = planes_and_out
    proj[...] = quarters[:, : 5 * ROWS]

    def put(position, value):
        count = value.shape[0] // ROWS
        out[ROWS * position : ROWS * (position + count)] = value.astype(BF16)

    def quarter(x, start, stop):
        return quarters[x, ROWS * start : ROWS * stop].astype(F32)

    for node in range(2):
        put(4 * node, quarter(2 * node, 5, 9) + quarter(2 * node + 1, 5, 9))
    if planes:
        (planes,) = planes
        pair = 2 * (lax.axis_index("zl") // 2)
        second, first = slice(0, 2 * ROWS), slice(2 * ROWS, 3 * ROWS)
        put(8, planes[pair, second].astype(F32) + planes[pair + 1, second].astype(F32))
        put(10, sum((planes[plane, first].astype(F32) for plane in range(1, 4)), planes[0, first].astype(F32)))
        put(11, jnp.zeros((3 * ROWS, R), F32))
    else:
        put(8, quarter_sum(quarters, 9, 15))
    node = lax.axis_index("x") // 2
    four = slice(4 * ROWS, 5 * ROWS)
    put(14, apart(quarters[2 * node, four], quarters[2 * node + 1, four], coupling, 4))


def of_core(ref, core, *positions):
    return jnp.concatenate(
        [ref[2 * y + core, ROWS * p : ROWS * (p + 1)] for p in positions for y in range(HALF)], axis=0
    )


def gathered(ref, position):
    rows = slice(ROWS * position, ROWS * (position + 1))
    return jnp.concatenate([ref[2 * y + c, rows] for c in range(2) for y in range(HALF)], axis=0)


def apart(left, right, coupling, level):
    return dot_t(jnp.concatenate([left, right], axis=1), coupling[level, 0])


def levels_kernel(quarters, mixed, coupling, out, keep):
    def proj(x, level):
        return quarters[x, ROWS * level : ROWS * (level + 1)]

    def blocks(core, *positions):
        return jnp.concatenate([of_core(mixed, core, *positions), of_core(mixed, core, *(p + 1 for p in positions))], axis=1)

    sums = []
    for node in range(2):
        pair = jnp.concatenate([proj(2 * node, 4), proj(2 * node + 1, 4)], axis=1)
        updates = []
        for core in range(2):
            both = dot_t(pair, blocks(core, 4 * node, 4 * node + 2))
            updates += [both[:, :R], both[:, R:]]
        sums.append(
            [
                proj(2 * node, l).astype(F32) + proj(2 * node + 1, l).astype(F32) - updates[l]
                for l in range(4)
            ]
        )
    left, right = sums[0][3].astype(BF16), sums[1][3].astype(BF16)
    pair = jnp.concatenate([left, right], axis=1)
    both = dot_t(pair, blocks(0, 8, 10))
    two = (sums[0][2] + sums[1][2] - dot_t(pair, blocks(0, 12))).astype(BF16)
    lower = dot_t(two, of_core(mixed, 1, 8, 9))
    one = (sums[0][1] + sums[1][1] - both[:, R:] - lower[:, R:]).astype(BF16)
    zero = sums[0][0] + sums[1][0] - both[:, :R] - lower[:, :R] - dot_t(one, of_core(mixed, 1, 10))
    result = jnp.concatenate([zero.astype(BF16), one, two], axis=0)
    for copy in range(8):
        out[copy] = result
    keep[...] = apart(left, right, coupling, 3).astype(BF16)


def corr_kernel(planes, coupling, keep, out):
    def proj(plane, level):
        return planes[plane, ROWS * level : ROWS * (level + 1)]

    def over(level, first, count):
        return sum(
            (proj(first + plane, level).astype(F32) for plane in range(1, count)), proj(first, level).astype(F32)
        ).astype(BF16)

    z = lax.axis_index("zh") * 4 + lax.axis_index("zl")
    pair, quad = 2 * (z // 2), 4 * (z // 4)
    zero = apart(over(0, 0, 4), over(0, 4, 4), coupling, 0).astype(BF16)
    one = apart(over(1, quad, 2), over(1, quad + 2, 2), coupling, 1).astype(BF16)
    two = apart(proj(pair, 2), proj(pair + 1, 2), coupling, 2).astype(BF16)
    result = jnp.concatenate([zero, one, two, keep[...]], axis=0)
    for copy in range(2 * HALF):
        out[copy] = result


def apply_kernel(rhs, bases, mixed, corr, out, here, sems):
    levels = [gathered(corr, level) for level in range(4)] + [gathered(mixed, 14)]
    everything = jnp.concatenate(levels, axis=1)
    width = rhs.shape[1] // OUT_CHUNKS
    copies = []
    for chunk in range(OUT_CHUNKS):
        columns = slice(chunk * width, (chunk + 1) * width)
        update = dot(everything, bases[:, :, columns].reshape(5 * R, width))
        here[:, columns] = (rhs[:, columns].astype(F32) - update).astype(BF16)
        columns = pl.ds(chunk * width, width)
        copies.append(pltpu.make_async_copy(here.at[:, columns], out.at[:, columns], sems.at[chunk]))
        copies[-1].start()
    for copy in copies:
        copy.wait()


def apply_levels(rhs, *arrays):
    whole = pl.BlockSpec(memory_space=pltpu.VMEM)
    return pl.pallas_call(
        apply_kernel,
        in_specs=[whole] * (1 + len(arrays)),
        out_specs=pl.BlockSpec(memory_space=pltpu.HBM),
        out_shape=jax.ShapeDtypeStruct(rhs.shape, BF16),
        scratch_shapes=[pltpu.VMEM(rhs.shape, BF16), pltpu.SemaphoreType.DMA((OUT_CHUNKS,))],
        compiler_params=pltpu.CompilerParams(vmem_limit_bytes=VMEM_LIMIT),
    )(rhs, *arrays)


def on_device(rhs, bases, coupling):
    group = ("y", "c")
    swap = [(0, 1), (1, 0)]
    exchange = functools.partial(lax.all_to_all, split_axis=0, concat_axis=0)

    mine, other = project(project_kernel, 2, rhs, bases)
    theirs = lax.ppermute(other, "c", swap)
    (parts,) = local_call(chip_kernel, [(mine.shape, BF16)], mine, theirs)

    def reduce_and_mix(core, rhs, bases, parts, coupling):
        if not core:
            (parts,) = project(own_kernel, 1, rhs, bases, parts)
        parts = exchange(parts, "y")
        couple = functools.partial(couple_kernel, core)
        (quarters,) = local_call(couple, [((4, 15 * ROWS, R), BF16)], parts, coupling)
        quarters = exchange(quarters, "x")
        planes = []
        if core:
            planes = local_call(plane_kernel, [((4, 3 * ROWS, R), BF16)], quarters)
            planes = [exchange(planes[0], "zl")]
        shapes = [((4, 5 * ROWS, R), BF16), ((15 * ROWS, R), BF16)]
        return local_call(nodes_kernel, shapes, quarters, coupling, *planes)

    proj, mixed = lax.cond(
        lax.axis_index("c") == 1,
        functools.partial(reduce_and_mix, 1),
        functools.partial(reduce_and_mix, 0),
        rhs,
        bases,
        parts,
        coupling,
    )
    mixed = lax.all_gather(mixed, group)
    lower, keep = local_call(
        levels_kernel,
        [((8, 3 * ROWS, R), BF16), ((ROWS, R), BF16)],
        proj,
        mixed,
        coupling,
    )
    lower = exchange(lower, ("zh", "zl"))
    (corr,) = local_call(corr_kernel, [((2 * HALF, 4 * ROWS, R), BF16)], lower, coupling, keep)
    return apply_levels(rhs, bases, mixed, exchange(corr, group))


def solution(mesh):
    names = ("zh", "zl", "x", "y", "c")
    split = Mesh(mesh.devices.reshape(2, 4, 4, 8, 2), names)
    return jax.shard_map(
        on_device,
        mesh=split,
        in_specs=(P(None, names), P(None, None, names), P(None, names, None, None)),
        out_specs=P(None, names),
        check_vma=False,
    )
```

```python
import functools

import jax
import jax.numpy as jnp
from jax import lax
from jax.experimental import pallas as pl
from jax.experimental.pallas import tpu as pltpu
from jax.sharding import Mesh
from jax.sharding import PartitionSpec as P


ROWS = 16
R = 128
CHUNKS = 2
OUT_CHUNKS = 2
HALF = 8
F32 = jnp.float32
BF16 = jnp.bfloat16
VMEM_LIMIT = 40 * 1024 * 1024
PROJECT_VMEM_LIMIT = 53 * 1024 * 1024


def dot_t(a, b):
    return lax.dot_general(a, b, (((1,), (1,)), ((), ())), preferred_element_type=F32)


def dot(a, b):
    return jnp.dot(a, b, preferred_element_type=F32)


def load(rhs, rhs_rows, bases, stack, sems):
    width = rhs.shape[1] // CHUNKS
    copies = []
    for chunk in range(CHUNKS):
        columns = pl.ds(chunk * width, width)
        count = rhs_rows.stop - rhs_rows.start
        source = rhs.at[pl.ds(rhs_rows.start, count), columns]
        copies.append([pltpu.make_async_copy(source, stack.at[pl.ds(0, count), columns], sems.at[0, chunk])])
        for level in range(5):
            rows = pl.ds(count + level * R, R)
            copies[chunk].append(
                pltpu.make_async_copy(
                    bases.at[level, :, columns], stack.at[rows, columns], sems.at[level + 1, chunk]
                )
            )
        for copy in copies[chunk]:
            copy.start()
    return copies


def multiply(copies, stack, products):
    width = stack.shape[1] // CHUNKS
    for chunk in range(CHUNKS):
        columns = slice(chunk * width, (chunk + 1) * width)
        for copy in copies[chunk]:
            copy.wait()
        for acc, lefts, rights in products:
            value = dot_t(
                stack[lefts.start * R : lefts.stop * R, columns], stack[rights.start * R : rights.stop * R, columns]
            )
            if chunk == 0:
                acc[: value.shape[0]] = value
            else:
                acc[: value.shape[0]] += value


def tile(ref, row, column):
    return ref[row * R : (row + 1) * R, column * R : (column + 1) * R]


def rows_of(position):
    return slice(ROWS * position, ROWS * (position + 1))


def half_products(half, rhs, bases, stack, high, middle, low, sems, put):
    copies = load(rhs, slice(R * half, R * (half + 1)), bases, stack, sems)
    multiply(
        copies,
        stack,
        [(high, slice(0, 5), slice(4, 6)), (middle, slice(0, 3), slice(2, 4)), (low, slice(0, 1), slice(1, 2))],
    )
    places = [(low, 0, 0), (middle, 0, 0), (middle, 0, 1), (high, 0, 0), (high, 0, 1)]
    if half == 0:
        places += [(high, 1, 1), (high, 2, 1), (high, 1, 0), (high, 2, 0), (high, 3, 0)]
    else:
        places += [(high, 3, 1), (high, 4, 1), (middle, 1, 1), (middle, 2, 1), (middle, 1, 0)]
    for position, place in enumerate(places):
        put(position, tile(*place))


def project_kernel(rhs, bases, mine, other, stack, high, middle, low, sems):
    core = lax.axis_index("c")

    @pl.when(core == 0)
    def _():
        def put(position, value):
            other[:, rows_of(position), :] = value.astype(BF16).reshape(HALF, ROWS, R)

        half_products(1, rhs, bases, stack, high, middle, low, sems, put)
        mine[...] = jnp.zeros_like(mine)

    @pl.when(core == 1)
    def _():
        def put(position, zero, one):
            other[:, rows_of(position), :] = zero.astype(BF16).reshape(HALF, ROWS, R)
            mine[:, rows_of(position), :] = one.astype(BF16).reshape(HALF, ROWS, R)

        copies = load(rhs, slice(0, 2 * R), bases, stack, sems)
        multiply(
            copies,
            stack,
            [(high, slice(0, 6), slice(5, 7)), (middle, slice(0, 4), slice(3, 5)), (low, slice(0, 2), slice(2, 3))],
        )
        for level, (ref, column) in enumerate([(low, 0), (middle, 0), (middle, 1), (high, 0), (high, 1)]):
            put(level, tile(ref, 0, column), tile(ref, 1, column))
        put(5, tile(high, 2, 1), tile(high, 4, 1))
        put(6, tile(high, 3, 1), tile(high, 5, 1))
        put(7, tile(high, 2, 0), tile(middle, 2, 1))
        put(8, tile(high, 3, 0), tile(middle, 3, 1))
        put(9, tile(high, 4, 0), tile(middle, 2, 0))


def own_kernel(rhs, bases, theirs, out, stack, high, middle, low, sems):
    def put(position, value):
        rows = rows_of(position)
        out[:, rows, :] = (value.reshape(HALF, ROWS, R) + theirs[:, rows, :].astype(F32)).astype(BF16)

    half_products(0, rhs, bases, stack, high, middle, low, sems, put)


def project(kernel, outputs, rhs, bases, *theirs):
    hbm = pl.BlockSpec(memory_space=pltpu.HBM)
    whole = pl.BlockSpec(memory_space=pltpu.VMEM)
    return pl.pallas_call(
        kernel,
        in_specs=[hbm, hbm] + [whole] * len(theirs),
        out_specs=[whole] * outputs,
        out_shape=[jax.ShapeDtypeStruct((HALF, 10 * ROWS, R), BF16)] * outputs,
        scratch_shapes=[
            pltpu.VMEM((7 * R, rhs.shape[1]), BF16),
            pltpu.VMEM((6 * R, 2 * R), F32),
            pltpu.VMEM((4 * R, 2 * R), F32),
            pltpu.VMEM((2 * R, R), F32),
            pltpu.SemaphoreType.DMA((6, CHUNKS)),
        ],
        compiler_params=pltpu.CompilerParams(vmem_limit_bytes=PROJECT_VMEM_LIMIT),
    )(rhs, bases, *theirs)


def local_call(kernel, shapes, *arrays):
    whole = pl.BlockSpec(memory_space=pltpu.VMEM)
    return pl.pallas_call(
        kernel,
        in_specs=[whole] * len(arrays),
        out_specs=[whole] * len(shapes),
        out_shape=[jax.ShapeDtypeStruct(shape, dtype) for shape, dtype in shapes],
        compiler_params=pltpu.CompilerParams(vmem_limit_bytes=VMEM_LIMIT),
    )(*arrays)


def chip_kernel(mine, theirs, out):
    out[...] = (mine[...].astype(F32) + theirs[...].astype(F32)).astype(BF16)


def couple_kernel(parts, coupling, out):
    total = parts[0].astype(F32)
    for source in range(1, HALF):
        total += parts[source].astype(F32)
    total = total.astype(BF16)
    proj, gram = total[: 5 * ROWS], total[5 * ROWS :]
    levels = (4, 4, 3, 3, 3)
    mixed = [dot(gram[ROWS * p : ROWS * (p + 1)], coupling[level, 0]) for p, level in enumerate(levels)]
    halves = [m[:, R * half : R * (half + 1)].astype(BF16) for m in mixed for half in (0, 1)]
    whole = jnp.concatenate([proj] + halves, axis=0)
    for copy in range(4):
        out[copy] = whole


def couple_one_kernel(parts, coupling, first, planes):
    total = parts[0].astype(F32)
    for source in range(1, HALF):
        total += parts[source].astype(F32)
    total = total.astype(BF16)
    gram = total[5 * ROWS :]
    mixed = [dot(gram[ROWS * p : ROWS * (p + 1)], coupling[level, 0]) for p, level in enumerate((4, 4, 2, 2, 1))]
    halves = [[m[:, :R].astype(BF16), m[:, R:].astype(BF16)] for m in mixed]
    first[...] = jnp.concatenate([total[: 5 * ROWS]] + halves[0] + halves[1], axis=0)
    for plane in range(4):
        planes[plane] = jnp.concatenate(
            [halves[2][plane % 2], halves[3][plane % 2], halves[4][plane // 2]], axis=0
        )


def join_kernel(first, planes, out):
    pair = 2 * (lax.axis_index("zl") // 2)
    two, one = slice(0, 2 * ROWS), slice(2 * ROWS, 3 * ROWS)
    seconds = planes[pair, two].astype(F32) + planes[pair + 1, two].astype(F32)
    firsts = sum((planes[plane, one].astype(F32) for plane in range(1, 4)), planes[0, one].astype(F32))
    whole = jnp.concatenate([first[...], seconds.astype(BF16), firsts.astype(BF16)], axis=0)
    for copy in range(4):
        out[copy] = whole


def quarter_sum(quarters, start, stop):
    rows = slice(ROWS * start, ROWS * stop)
    return sum((quarters[x, rows].astype(F32) for x in range(1, 4)), quarters[0, rows].astype(F32))


def nodes_kernel(core, quarters, coupling, proj, out):
    proj[...] = quarters[:, : 5 * ROWS]

    def put(position, value):
        count = value.shape[0] // ROWS
        out[ROWS * position : ROWS * (position + count)] = value.astype(BF16)

    def quarter(x, start, stop):
        return quarters[x, ROWS * start : ROWS * stop].astype(F32)

    for node in range(2):
        put(4 * node, quarter(2 * node, 5, 9) + quarter(2 * node + 1, 5, 9))
    if core:
        put(8, quarter_sum(quarters, 9, 12))
        put(11, jnp.zeros((3 * ROWS, R), F32))
    else:
        put(8, quarter_sum(quarters, 9, 15))
    node = lax.axis_index("x") // 2
    four = slice(4 * ROWS, 5 * ROWS)
    put(14, apart(quarters[2 * node, four], quarters[2 * node + 1, four], coupling, 4))


def of_core(ref, core, *positions):
    return jnp.concatenate(
        [ref[2 * y + core, ROWS * p : ROWS * (p + 1)] for p in positions for y in range(HALF)], axis=0
    )


def gathered(ref, position):
    rows = slice(ROWS * position, ROWS * (position + 1))
    return jnp.concatenate([ref[2 * y + c, rows] for c in range(2) for y in range(HALF)], axis=0)


def apart(left, right, coupling, level):
    return dot_t(left, coupling[level, 0][:, :R]) + dot_t(right, coupling[level, 0][:, R:])


def levels_kernel(quarters, mixed, coupling, out, keep):
    def proj(x, level):
        return quarters[x, ROWS * level : ROWS * (level + 1)]

    sums = []
    for node in range(2):
        left, right = proj(2 * node, 4), proj(2 * node + 1, 4)
        base = 4 * node
        updates = []
        for core in range(2):
            both = dot_t(left, of_core(mixed, core, base, base + 2))
            both += dot_t(right, of_core(mixed, core, base + 1, base + 3))
            updates += [both[:, :R], both[:, R:]]
        sums.append(
            [
                proj(2 * node, l).astype(F32) + proj(2 * node + 1, l).astype(F32) - updates[l]
                for l in range(4)
            ]
        )
    left, right = sums[0][3].astype(BF16), sums[1][3].astype(BF16)
    both = dot_t(left, of_core(mixed, 0, 8, 10)) + dot_t(right, of_core(mixed, 0, 9, 11))
    update = dot_t(left, of_core(mixed, 0, 12)) + dot_t(right, of_core(mixed, 0, 13))
    two = (sums[0][2] + sums[1][2] - update).astype(BF16)
    lower = dot_t(two, of_core(mixed, 1, 8, 9))
    one = (sums[0][1] + sums[1][1] - both[:, R:] - lower[:, R:]).astype(BF16)
    zero = sums[0][0] + sums[1][0] - both[:, :R] - lower[:, :R] - dot_t(one, of_core(mixed, 1, 10))
    result = jnp.concatenate([zero.astype(BF16), one, two], axis=0)
    for copy in range(8):
        out[copy] = result
    keep[...] = apart(left, right, coupling, 3).astype(BF16)


def corr_kernel(planes, coupling, keep, out):
    def proj(plane, level):
        return planes[plane, ROWS * level : ROWS * (level + 1)]

    def over(level, first, count):
        return sum(
            (proj(first + plane, level).astype(F32) for plane in range(1, count)), proj(first, level).astype(F32)
        ).astype(BF16)

    z = lax.axis_index("zh") * 4 + lax.axis_index("zl")
    pair, quad = 2 * (z // 2), 4 * (z // 4)
    zero = apart(over(0, 0, 4), over(0, 4, 4), coupling, 0).astype(BF16)
    one = apart(over(1, quad, 2), over(1, quad + 2, 2), coupling, 1).astype(BF16)
    two = apart(proj(pair, 2), proj(pair + 1, 2), coupling, 2).astype(BF16)
    result = jnp.concatenate([zero, one, two, keep[...]], axis=0)
    for copy in range(2 * HALF):
        out[copy] = result


def apply_kernel(rhs, bases, mixed, corr, out, here, sems):
    levels = [gathered(corr, level) for level in range(4)] + [gathered(mixed, 14)]
    everything = jnp.concatenate(levels, axis=1)
    width = rhs.shape[1] // OUT_CHUNKS
    copies = []
    for chunk in range(OUT_CHUNKS):
        columns = slice(chunk * width, (chunk + 1) * width)
        update = dot(everything, bases[:, :, columns].reshape(5 * R, width))
        here[:, columns] = (rhs[:, columns].astype(F32) - update).astype(BF16)
        columns = pl.ds(chunk * width, width)
        copies.append(pltpu.make_async_copy(here.at[:, columns], out.at[:, columns], sems.at[chunk]))
        copies[-1].start()
    for copy in copies:
        copy.wait()


def apply_levels(rhs, *arrays):
    whole = pl.BlockSpec(memory_space=pltpu.VMEM)
    return pl.pallas_call(
        apply_kernel,
        in_specs=[whole] * (1 + len(arrays)),
        out_specs=pl.BlockSpec(memory_space=pltpu.HBM),
        out_shape=jax.ShapeDtypeStruct(rhs.shape, BF16),
        scratch_shapes=[pltpu.VMEM(rhs.shape, BF16), pltpu.SemaphoreType.DMA((OUT_CHUNKS,))],
        compiler_params=pltpu.CompilerParams(vmem_limit_bytes=VMEM_LIMIT),
    )(rhs, *arrays)


def on_device(rhs, bases, coupling):
    group = ("y", "c")
    swap = [(0, 1), (1, 0)]
    exchange = functools.partial(lax.all_to_all, split_axis=0, concat_axis=0)

    mine, other = project(project_kernel, 2, rhs, bases)
    theirs = lax.ppermute(other, "c", swap)
    (parts,) = local_call(chip_kernel, [(mine.shape, BF16)], mine, theirs)

    def reduce_and_mix(core, rhs, bases, parts, coupling):
        if not core:
            (parts,) = project(own_kernel, 1, rhs, bases, parts)
        parts = exchange(parts, "y")
        if core:
            shapes = [((9 * ROWS, R), BF16), ((4, 3 * ROWS, R), BF16)]
            first, planes = local_call(couple_one_kernel, shapes, parts, coupling)
            planes = exchange(planes, "zl")
            (quarters,) = local_call(join_kernel, [((4, 12 * ROWS, R), BF16)], first, planes)
        else:
            (quarters,) = local_call(couple_kernel, [((4, 15 * ROWS, R), BF16)], parts, coupling)
        quarters = exchange(quarters, "x")
        shapes = [((4, 5 * ROWS, R), BF16), ((15 * ROWS, R), BF16)]
        return local_call(functools.partial(nodes_kernel, core), shapes, quarters, coupling)

    proj, mixed = lax.cond(
        lax.axis_index("c") == 1,
        functools.partial(reduce_and_mix, 1),
        functools.partial(reduce_and_mix, 0),
        rhs,
        bases,
        parts,
        coupling,
    )
    mixed = lax.all_gather(mixed, group)
    lower, keep = local_call(
        levels_kernel,
        [((8, 3 * ROWS, R), BF16), ((ROWS, R), BF16)],
        proj,
        mixed,
        coupling,
    )
    lower = exchange(lower, ("zh", "zl"))
    (corr,) = local_call(corr_kernel, [((2 * HALF, 4 * ROWS, R), BF16)], lower, coupling, keep)
    return apply_levels(rhs, bases, mixed, exchange(corr, group))


def solution(mesh):
    names = ("zh", "zl", "x", "y", "c")
    split = Mesh(mesh.devices.reshape(2, 4, 4, 8, 2), names)
    return jax.shard_map(
        on_device,
        mesh=split,
        in_specs=(P(None, names), P(None, None, names), P(None, names, None, None)),
        out_specs=P(None, names),
        check_vma=False,
    )
```
